512 devices in a mesh: rows: 64 (over x, z), grp: 8 (over y, core).
Axes of the slice: x: 4, y: 4, z: 16, core: 2. Of those that a mesh axis runs over, the one named last changes fastest.
Arguments:
- activations: bfloat16 [131072, 8192], P(('rows', 'grp')), may hold values from -120 to 120
- start_basis: bfloat16 [131072, 64], P(('rows', 'grp')), may hold values from -6 to 6
Outputs:
- new_basis: float32 [131072, 64], P(('rows', 'grp'))
- rfactor: float32 [64, 64], replicated
The draws below stay inside these ranges and needn't reach their ends.
All inputs are finite; a program needn't handle non-finite values.
Results may differ from the reference program's by a relative error of at most 0.0029.
Values may be sent and summed in bfloat16 or wider, within the bound.
A program may use at most 64 MiB of HBM per device.

```python
import jax
import jax.numpy as jnp
from jax import lax

D = 8192
K = 64
TOTAL_ROWS = 131072


def draw_activations(key, part):
    key = jax.random.fold_in(key, 11)
    key_noise, key_rows, key_cols = jax.random.split(key, 3)
    row_scale = jnp.exp(jax.random.uniform(key_rows, (TOTAL_ROWS, 1), jnp.float32, 0.0, jnp.log(10.0)))
    col_scale = jnp.exp(jax.random.uniform(key_cols, (1, D), jnp.float32, jnp.log(0.3), jnp.log(3.0)))
    values = jax.random.truncated_normal(key_noise, -4.0, 4.0, (TOTAL_ROWS, D), jnp.float32)
    return (values * row_scale * col_scale).astype(jnp.bfloat16)


def shard_levels(stream_key, dims, shards, low, high):
    gain, own = 1.0, jax.random.fold_in(stream_key, 6)
    for dim, blocks in shards:
        draws = jnp.exp(jax.random.uniform(jax.random.fold_in(own, dim), (blocks,), jnp.float32, low / len(shards), high / len(shards)))
        gain = gain * jnp.repeat(draws, dims[dim] // blocks).reshape([-1 if axis == dim else 1 for axis in range(len(dims))])
    return gain


def normal_values(rng, shape, spread, bound, cuts=(), dtype=jnp.bfloat16):
    loudness = shard_levels(rng, shape, cuts, -0.22, 0.18) if cuts else 1.0
    drawn = jax.random.normal(rng, shape, jnp.float32) * spread * loudness
    return jnp.minimum(jnp.maximum(drawn, -bound), bound).astype(dtype)


def setup_inputs(seed: int = 0) -> dict:
    streams_of = jax.random.split(jax.random.key(seed), 3)
    activations = draw_activations(jax.random.fold_in(streams_of[2], 71), 0)
    start_basis = normal_values(streams_of[1], (TOTAL_ROWS, K), 1.0, 6.0, ((0, 512),))
    return {"activations": activations, "start_basis": start_basis}


def reference(activations, start_basis):
    projected = jnp.dot(activations.T.astype(jnp.float32), start_basis.astype(jnp.float32), preferred_element_type=jnp.float32) / jnp.sqrt(jnp.float32(TOTAL_ROWS))
    projected = projected.astype(jnp.bfloat16)
    image = jnp.dot(activations.astype(jnp.float32), projected.astype(jnp.float32), preferred_element_type=jnp.float32) / jnp.sqrt(jnp.float32(D))
    gram = jnp.dot(image.T, image, precision=lax.Precision.HIGHEST) / jnp.float32(TOTAL_ROWS)
    lower = jnp.linalg.cholesky(gram)
    new_basis = jax.scipy.linalg.solve_triangular(lower, image.T, lower=True).T
    return (new_basis, lower.T)
```

```python
import functools
import math

import jax
import jax.numpy as jnp
from jax import lax
from jax.experimental import pallas as pl
from jax.experimental.pallas import tpu as pltpu
from jax.sharding import PartitionSpec as P

MESH = pl.DeviceIdType.MESH
F32 = jnp.float32
BF16 = jnp.bfloat16
ROWS, D, K = 256, 8192, 64
TOTAL = 131072
CHUNK = 512


def comm_kernel(a_hbm, s_hbm, img_ref, gram_ref, a_v, s_v, other, land_c, r1, land_1, r2, land_2, r3, land_z, pall,
                g_own, land_g, g_z, g_all,
                load_sem, c_send, c_recv, s1_send, s1_recv, s2_send, s2_recv, z_send, z_recv,
                zg_send, zg_recv, xy_send, xy_recv, f_send, f_recv,
                g1_send, g1_recv, g2_send, g2_recv, g3_send, g3_recv):
    r = lax.axis_index("rows")
    g = lax.axis_index("grp")
    x, z = r // 16, r % 16
    y, c = g // 2, g % 2

    def dev(xx, yy, zz, cc):
        return (xx * 16 + zz, yy * 2 + cc)

    partner = dev(x, y, z, 1 - c)

    def plane(k):
        return (x + k // 8) % 4, (y + (k // 2) % 4) % 4, (c + k % 2) % 2

    def remote(src, dst, ss, rs, target):
        return pltpu.make_async_remote_copy(src_ref=src, dst_ref=dst, send_sem=ss, recv_sem=rs, device_id=target,
                                            device_id_type=MESH)

    pltpu.make_async_copy(s_hbm, s_v, load_sem.at[16]).start()
    order = []
    for half in (1, 0):
        for j in range(8):
            order.append((half, j))
    for half, j in order:
        ch = (c if half == 0 else 1 - c) * 8 + j
        pltpu.make_async_copy(a_hbm.at[:, pl.ds(pl.multiple_of(ch * CHUNK, CHUNK), CHUNK)], a_v.at[ch], load_sem.at[ch]).start()

    bar = pltpu.get_barrier_semaphore()

    @pl.loop(1, 32)
    def _(k):
        xx, yy, cc = plane(k)
        pl.semaphore_signal(bar, inc=1, device_id=dev(xx, yy, z, cc), device_id_type=MESH)

    @pl.loop(1, 16)
    def _(k):
        pl.semaphore_signal(bar, inc=1, device_id=dev(x, y, (z + k) % 16, c), device_id_type=MESH)

    pltpu.make_async_copy(s_hbm, s_v, load_sem.at[16]).wait()
    st = s_v[...].astype(F32).T.astype(BF16)

    def partial(ch, j, dst):
        pltpu.make_async_copy(a_hbm.at[:, pl.ds(0, CHUNK)], a_v.at[ch], load_sem.at[ch]).wait()
        part = jnp.dot(st, a_v[ch], preferred_element_type=F32)
        q, a = j // 4, j % 4
        for s in range(4):
            for b in range(4):
                dst[q * 4 + s, a, b] = part[16 * s:16 * s + 16, 128 * b:128 * b + 128]

    @pl.loop(0, 8)
    def _(j):
        partial((1 - c) * 8 + j, j, other)

    pl.semaphore_wait(bar, 46)

    c_copies = [remote(other.at[i], land_c.at[i], c_send.at[i], c_recv.at[i], partner) for i in range(8)]
    for cp in c_copies:
        cp.start()

    @pl.loop(0, 8)
    def _(j):
        partial(c * 8 + j, j, r1)

    me_a = (x, y)
    me_b = (y, x)

    def first_peer(q, k):
        return dev((x + k) % 4, y, z, c) if q == 0 else dev(x, (y + k) % 4, z, c)

    def second_peer(q, k):
        return first_peer(1 - q, k)

    copies_1 = {}
    for s in range(4):
        for q in range(2):
            i = q * 4 + s
            c_copies[i].wait_recv()
            r1[i] = r1[i] + land_c[i]
            for k in (1, 2, 3):
                n = i * 3 + k - 1
                cp = remote(r1.at[i, (me_a[q] + k) % 4], land_1.at[i, k - 1], s1_send.at[n], s1_recv.at[n], first_peer(q, k))
                cp.start()
                copies_1[i, k] = cp
    copies_2 = {}
    for s in range(4):
        for q in range(2):
            i = q * 4 + s
            for k in (1, 2, 3):
                copies_1[i, k].wait_recv()
            r2[i] = (r1[i, me_a[q]] + land_1[i, 0]) + (land_1[i, 1] + land_1[i, 2])
            for k in (1, 2, 3):
                n = i * 3 + k - 1
                cp = remote(r2.at[i, (me_b[q] + k) % 4], land_2.at[i, k - 1], s2_send.at[n], s2_recv.at[n], second_peer(q, k))
                cp.start()
                copies_2[i, k] = cp

    def z_copy(i, slot):
        zo = 4 * (i % 4) + 2 * (i // 4) + c
        return zo, remote(r3.at[i], land_z.at[slot], z_send.at[i], z_recv.at[slot], dev(x, y, zo, c))

    for s in range(4):
        for q in range(2):
            i = q * 4 + s
            for k in (1, 2, 3):
                copies_2[i, k].wait_recv()
            r3[i] = (r2[i, me_b[q]] + land_2[i, 0]) + (land_2[i, 1] + land_2[i, 2])
            zo = 4 * s + 2 * q + c

            @pl.when(zo != z)
            def _(i=i, zo=zo):
                z_copy(i, (zo - z + 16) % 16)[1].start()

    my_s, my_q = z // 4, (z % 4) // 2
    my_i = my_q * 4 + my_s
    owner = z % 2 == c

    def place(q):
        return (c * 2 + q) * 16 + jnp.where(q == 0, x * 4 + y, y * 4 + x)

    def zg_copy(k):
        here = pall.at[place(my_q), my_s]
        return remote(here, here, zg_send.at[k], zg_recv.at[my_i], dev(x, y, (z + k) % 16, c))

    @pl.when(owner)
    def _():
        total = r3[my_i]
        for k in range(1, 16):
            pltpu.make_async_copy(land_z.at[k], land_z.at[k], z_recv.at[k]).wait()
        for k in range(1, 16):
            total = total + land_z[k]
        pall[place(my_q), my_s] = (total * (1.0 / math.sqrt(TOTAL))).astype(BF16)

        @pl.loop(1, 16)
        def _(k):
            zg_copy(k).start()

    def xy_copy(k, q, s):
        here = pall.at[place(q), s]
        return remote(here, here, xy_send.at[k, q], xy_recv.at[k, q], dev((x + k // 4) % 4, (y + k % 4) % 4, z, c))

    for j in range(8):
        off = jnp.where(owner, (0, 2, 14, 4, 12, 6, 10, 8)[j], (1, 15, 3, 13, 5, 11, 7, 9)[j])
        zz = (z + off) % 16
        s, q = zz // 4, (zz % 4) // 2

        @pl.when(off != 0)
        def _(s=s, q=q):
            here = pall.at[place(q), s]
            pltpu.make_async_copy(here, here, zg_recv.at[q * 4 + s]).wait()

        @pl.loop(1, 16)
        def _(k, q=q, s=s):
            xy_copy(k, q, s).start()

    def forward(k, q):
        xx, yy = (x - k // 4 + 4) % 4, (y - k % 4 + 4) % 4
        p = (c * 2 + q) * 16 + (xx * 4 + yy if q == 0 else yy * 4 + xx)
        return p, remote(pall.at[p], pall.at[p], f_send, f_recv, partner)

    for q in range(2):
        forward(0, q)[1].start()

    @pl.loop(1, 16)
    def _(k):
        for q in range(2):
            p, cp = forward(k, q)
            pltpu.make_async_copy(pall.at[p], pall.at[p], xy_recv.at[k, q]).wait()
            cp.start()

    def image_part(half, acc):
        def body(j, acc):
            ch = half * 8 + j
            pt = jnp.concatenate([pall[ch * 4 + b].reshape(64, 128) for b in range(4)], axis=1)
            return acc + lax.dot_general(a_v[ch], pt, (((1,), (1,)), ((), ())), preferred_element_type=F32)
        return lax.fori_loop(0, 8, body, acc)

    acc = image_part(c, jnp.zeros((ROWS, K), F32))
    theirs = pall.at[pl.ds((1 - c) * 32, 32)]
    pltpu.make_async_copy(theirs, theirs, f_recv).wait()
    acc = image_part(1 - c, acc)
    img = acc * (1.0 / math.sqrt(D))
    img_ref[...] = img
    gram = lax.dot_general(img, img, (((0,), (0,)), ((), ())), precision=lax.Precision.HIGHEST, preferred_element_type=F32)
    gram = gram * (1.0 / TOTAL)

    for m in range(32):
        g_own[m] = gram[2 * m:2 * m + 2, :]
    me = (x * 4 + y) * 2 + c

    def g1_copy(k):
        xx, yy, cc = plane(k)
        return remote(g_own.at[(xx * 4 + yy) * 2 + cc], land_g.at[k], g1_send.at[k], g1_recv.at[k], dev(xx, yy, z, cc))

    @pl.loop(1, 32)
    def _(k):
        g1_copy(k).start()

    tot = g_own[me]
    for k in range(1, 32):
        g1_copy(k).wait_recv()
    for k in range(1, 32):
        tot = tot + land_g[k]
    g_z[z] = tot

    def g2_copy(k, zs):
        return remote(g_z.at[zs], g_z.at[zs], g2_send.at[k], g2_recv.at[zs], dev(x, y, (z + k) % 16, c))

    @pl.loop(1, 16)
    def _(k):
        g2_copy(k, z).start()

    @pl.loop(1, 16)
    def _(k):
        g2_copy(k, (z + k) % 16).wait_recv()

    tot = g_z[0]
    for k in range(1, 16):
        tot = tot + g_z[k]
    g_all[me] = tot

    def g3_copy(k):
        xx, yy, cc = plane(k)
        return remote(g_all.at[me], g_all.at[me], g3_send.at[k], g3_recv.at[me], dev(xx, yy, z, cc))

    @pl.loop(1, 32)
    def _(k):
        g3_copy(k).start()

    @pl.loop(1, 32)
    def _(k):
        xx, yy, cc = plane(k)
        m = (xx * 4 + yy) * 2 + cc
        pltpu.make_async_copy(g_all.at[m], g_all.at[m], g3_recv.at[m]).wait()

    gram_ref[...] = g_all[...]

    for cp in c_copies:
        cp.wait_send()
    for i in range(8):
        for k in (1, 2, 3):
            copies_1[i, k].wait_send()
            copies_2[i, k].wait_send()
    for i in range(8):
        @pl.when(4 * (i % 4) + 2 * (i // 4) + c != z)
        def _(i=i):
            z_copy(i, 1)[1].wait_send()

    @pl.when(owner)
    def _():
        @pl.loop(1, 16)
        def _(k):
            zg_copy(k).wait_send()

    @pl.loop(1, 16)
    def _(k):
        for q in range(2):
            pltpu.make_async_copy(pall.at[q], pall.at[q], xy_send.at[k, q]).wait()
        g2_copy(k, z).wait_send()

    pltpu.make_async_copy(theirs, theirs, f_send).wait()

    @pl.loop(1, 32)
    def _(k):
        g1_copy(k).wait_send()
        g3_copy(k).wait_send()


def comm(activations, start_basis):
    dma = pltpu.SemaphoreType.DMA
    return pl.pallas_call(
        comm_kernel,
        out_shape=(jax.ShapeDtypeStruct((ROWS, K), F32), jax.ShapeDtypeStruct((32, 2, K), F32)),
        in_specs=[pl.BlockSpec(memory_space=pl.ANY)] * 2,
        out_specs=(pl.BlockSpec(memory_space=pltpu.VMEM),) * 2,
        scratch_shapes=[
            pltpu.VMEM((16, ROWS, CHUNK), BF16),
            pltpu.VMEM((ROWS, K), BF16),
            pltpu.VMEM((8, 4, 4, 16, 128), F32),
            pltpu.VMEM((8, 4, 4, 16, 128), F32),
            pltpu.VMEM((8, 4, 4, 16, 128), F32),
            pltpu.VMEM((8, 3, 4, 16, 128), F32),
            pltpu.VMEM((8, 4, 16, 128), F32),
            pltpu.VMEM((8, 3, 16, 128), F32),
            pltpu.VMEM((8, 16, 128), F32),
            pltpu.VMEM((16, 16, 128), F32),
            pltpu.VMEM((64, 4, 16, 128), BF16),
            pltpu.VMEM((32, 2, K), F32),
            pltpu.VMEM((32, 2, K), F32),
            pltpu.VMEM((16, 2, K), F32),
            pltpu.VMEM((32, 2, K), F32),
            dma((17,)), dma((8,)), dma((8,)), dma((24,)), dma((24,)), dma((24,)), dma((24,)), dma((8,)), dma((16,)),
            dma((16,)), dma((8,)), dma((16, 2)), dma((16, 2)), dma, dma,
            dma((32,)), dma((32,)), dma((16,)), dma((16,)), dma((32,)), dma((32,)),
        ],
        compiler_params=pltpu.CompilerParams(collective_id=0, has_side_effects=True, vmem_limit_bytes=40 << 20),
        cost_estimate=pl.CostEstimate(flops=4 * ROWS * D * K, bytes_accessed=ROWS * D * 2, transcendentals=0),
        name="reduce_project_gram",
    )(activations, start_basis)


def on_device(activations, start_basis):
    image, gram = comm(activations, start_basis)
    lower = jnp.linalg.cholesky(gram.reshape(K, K))
    new_basis = jax.scipy.linalg.solve_triangular(lower, image.T, lower=True).T
    return (new_basis, lower.T)


def solution(mesh):
    in_specs = (P(("rows", "grp"), None), P(("rows", "grp"), None))
    out_specs = (P(("rows", "grp"), None), P())
    return jax.shard_map(
        on_device, mesh=mesh, in_specs=in_specs, out_specs=out_specs, check_vma=False
    )
```

```python
import functools
import math

import jax
import jax.numpy as jnp
from jax import lax
from jax.experimental import pallas as pl
from jax.experimental.pallas import tpu as pltpu
from jax.sharding import PartitionSpec as P

MESH = pl.DeviceIdType.MESH
F32 = jnp.float32
BF16 = jnp.bfloat16
ROWS, D, K = 256, 8192, 64
TOTAL = 131072
CHUNK = 512


def comm_kernel(a_hbm, s_hbm, img_ref, gram_ref, a_v, s_v, other, land_c, r1, land_1, r2, land_2, r3, land_z, pall,
                g_own, land_g, g_z, g_all,
                load_sem, c_send, c_recv, s1_send, s1_recv, s2_send, s2_recv, z_send, z_recv,
                zg_send, zg_recv, xy_send, xy_recv, f_send, f_recv,
                g1_send, g1_recv, g2_send, g2_recv, g3_send, g3_recv):
    r = lax.axis_index("rows")
    g = lax.axis_index("grp")
    x, z = r // 16, r % 16
    y, c = g // 2, g % 2

    def dev(xx, yy, zz, cc):
        return (xx * 16 + zz, yy * 2 + cc)

    partner = dev(x, y, z, 1 - c)

    def plane(k):
        return (x + k // 8) % 4, (y + (k // 2) % 4) % 4, (c + k % 2) % 2

    def remote(src, dst, ss, rs, target):
        return pltpu.make_async_remote_copy(src_ref=src, dst_ref=dst, send_sem=ss, recv_sem=rs, device_id=target,
                                            device_id_type=MESH)

    bar = pltpu.get_barrier_semaphore()

    @pl.loop(1, 16)
    def _(k):
        pl.semaphore_signal(bar, inc=1, device_id=dev(x, y, (z + 8 + k // 2 * (1 - k % 2 * 2) + 16) % 16, c), device_id_type=MESH)

    @pl.loop(1, 32)
    def _(k):
        xx, yy, cc = plane(k)
        pl.semaphore_signal(bar, inc=1, device_id=dev(xx, yy, z, cc), device_id_type=MESH)

    pltpu.make_async_copy(s_hbm, s_v, load_sem.at[16]).start()
    order = []
    for half in (1, 0):
        for j in range(8):
            order.append((half, j))
    for half, j in order:
        ch = (c if half == 0 else 1 - c) * 8 + j
        pltpu.make_async_copy(a_hbm.at[:, pl.ds(pl.multiple_of(ch * CHUNK, CHUNK), CHUNK)], a_v.at[ch], load_sem.at[ch]).start()

    pltpu.make_async_copy(s_hbm, s_v, load_sem.at[16]).wait()
    st = s_v[...]

    def partial(ch, j, dst):
        pltpu.make_async_copy(a_hbm.at[:, pl.ds(0, CHUNK)], a_v.at[ch], load_sem.at[ch]).wait()
        part = jnp.dot(st, a_v[ch], preferred_element_type=F32)
        q, a = j // 4, j % 4
        for s in range(4):
            for b in range(4):
                dst[q * 4 + s, a, b] = part[16 * s:16 * s + 16, 128 * b:128 * b + 128]

    @pl.loop(0, 8)
    def _(j):
        partial((1 - c) * 8 + j, j, other)

    pl.semaphore_wait(bar, 46)

    c_copies = [remote(other.at[i], land_c.at[i], c_send.at[i], c_recv.at[i], partner) for i in range(8)]
    for cp in c_copies:
        cp.start()

    @pl.loop(0, 8)
    def _(j):
        partial(c * 8 + j, j, r1)

    me_a = (x, y)
    me_b = (y, x)

    def first_peer(q, k):
        return dev((x + k) % 4, y, z, c) if q == 0 else dev(x, (y + k) % 4, z, c)

    def second_peer(q, k):
        return first_peer(1 - q, k)

    copies_1 = {}
    for s in range(4):
        for q in range(2):
            i = q * 4 + s
            c_copies[i].wait_recv()
            r1[i] = r1[i] + land_c[i]
            for k in (1, 2, 3):
                n = i * 3 + k - 1
                cp = remote(r1.at[i, (me_a[q] + k) % 4], land_1.at[i, k - 1], s1_send.at[n], s1_recv.at[n], first_peer(q, k))
                cp.start()
                copies_1[i, k] = cp
    copies_2 = {}
    for s in range(4):
        for q in range(2):
            i = q * 4 + s
            for k in (1, 2, 3):
                copies_1[i, k].wait_recv()
            r2[i] = (r1[i, me_a[q]] + land_1[i, 0]) + (land_1[i, 1] + land_1[i, 2])
            for k in (1, 2, 3):
                n = i * 3 + k - 1
                cp = remote(r2.at[i, (me_b[q] + k) % 4], land_2.at[i, k - 1], s2_send.at[n], s2_recv.at[n], second_peer(q, k))
                cp.start()
                copies_2[i, k] = cp

    def z_copy(i, slot):
        zo = 4 * (i % 4) + 2 * (i // 4) + c
        return zo, remote(r3.at[i], land_z.at[slot], z_send.at[i], z_recv.at[slot], dev(x, y, zo, c))

    for s in range(4):
        for q in range(2):
            i = q * 4 + s
            for k in (1, 2, 3):
                copies_2[i, k].wait_recv()
            r3[i] = (r2[i, me_b[q]] + land_2[i, 0]) + (land_2[i, 1] + land_2[i, 2])
            zo = 4 * s + 2 * q + c

            @pl.when(zo != z)
            def _(i=i, zo=zo):
                z_copy(i, (zo - z + 16) % 16)[1].start()

    my_s, my_q = z // 4, (z % 4) // 2
    my_i = my_q * 4 + my_s
    owner = z % 2 == c

    def place(q):
        return (c * 2 + q) * 16 + jnp.where(q == 0, x * 4 + y, y * 4 + x)

    def zg_copy(k):
        here = pall.at[place(my_q), my_s]
        return remote(here, here, zg_send.at[k], zg_recv.at[my_i], dev(x, y, (z + k) % 16, c))

    @pl.when(owner)
    def _():
        total = r3[my_i]
        for k in range(1, 16):
            pltpu.make_async_copy(land_z.at[k], land_z.at[k], z_recv.at[k]).wait()
        for k in range(1, 16):
            total = total + land_z[k]
        pall[place(my_q), my_s] = (total * (1.0 / math.sqrt(TOTAL))).astype(BF16)

        @pl.loop(1, 16)
        def _(k):
            zg_copy(k).start()

    def xy_copy(k, q, s):
        here = pall.at[place(q), s]
        return remote(here, here, xy_send.at[k, q], xy_recv.at[k, q], dev((x + k // 4) % 4, (y + k % 4) % 4, z, c))

    for j in range(8):
        off = jnp.where(owner, (0, 2, 14, 4, 12, 6, 10, 8)[j], (1, 15, 3, 13, 5, 11, 7, 9)[j])
        zz = (z + off) % 16
        s, q = zz // 4, (zz % 4) // 2

        @pl.when(off != 0)
        def _(s=s, q=q):
            here = pall.at[place(q), s]
            pltpu.make_async_copy(here, here, zg_recv.at[q * 4 + s]).wait()

        @pl.loop(1, 16)
        def _(k, q=q, s=s):
            xy_copy(k, q, s).start()

    def forward(k, q):
        xx, yy = (x - k // 4 + 4) % 4, (y - k % 4 + 4) % 4
        p = (c * 2 + q) * 16 + (xx * 4 + yy if q == 0 else yy * 4 + xx)
        return p, remote(pall.at[p], pall.at[p], f_send, f_recv, partner)

    for q in range(2):
        forward(0, q)[1].start()

    @pl.loop(1, 16)
    def _(k):
        for q in range(2):
            p, cp = forward(k, q)
            pltpu.make_async_copy(pall.at[p], pall.at[p], xy_recv.at[k, q]).wait()
            cp.start()

    def image_part(half, acc):
        def body(j, acc):
            ch = half * 8 + j
            pt = jnp.concatenate([pall[ch * 4 + b].reshape(64, 128) for b in range(4)], axis=1)
            return acc + lax.dot_general(pt, a_v[ch], (((1,), (1,)), ((), ())), preferred_element_type=F32)
        return lax.fori_loop(0, 8, body, acc)

    acc = image_part(c, jnp.zeros((K, ROWS), F32))
    theirs = pall.at[pl.ds((1 - c) * 32, 32)]
    pltpu.make_async_copy(theirs, theirs, f_recv).wait()
    acc = image_part(1 - c, acc)
    img = acc * (1.0 / math.sqrt(D))
    img_ref[...] = img
    gram = lax.dot_general(img, img, (((1,), (1,)), ((), ())), precision=lax.Precision.HIGHEST, preferred_element_type=F32)
    gram = gram * (1.0 / TOTAL)

    for m in range(32):
        g_own[m] = gram[2 * m:2 * m + 2, :]
    me = (x * 4 + y) * 2 + c

    def g1_copy(k):
        xx, yy, cc = plane(k)
        return remote(g_own.at[(xx * 4 + yy) * 2 + cc], land_g.at[k], g1_send.at[k], g1_recv.at[k], dev(xx, yy, z, cc))

    @pl.loop(1, 32)
    def _(k):
        g1_copy(k).start()

    tot = g_own[me]
    for k in range(1, 32):
        g1_copy(k).wait_recv()
    for k in range(1, 32):
        tot = tot + land_g[k]
    g_z[z] = tot

    def g2_copy(k, zs):
        return remote(g_z.at[zs], g_z.at[zs], g2_send.at[k], g2_recv.at[zs], dev(x, y, (z + k) % 16, c))

    @pl.loop(1, 16)
    def _(k):
        g2_copy(k, z).start()

    @pl.loop(1, 16)
    def _(k):
        g2_copy(k, (z + k) % 16).wait_recv()

    tot = g_z[0]
    for k in range(1, 16):
        tot = tot + g_z[k]
    g_all[me] = tot

    def g3_copy(k):
        xx, yy, cc = plane(k)
        return remote(g_all.at[me], g_all.at[me], g3_send.at[k], g3_recv.at[me], dev(xx, yy, z, cc))

    @pl.loop(1, 32)
    def _(k):
        g3_copy(k).start()

    @pl.loop(1, 32)
    def _(k):
        xx, yy, cc = plane(k)
        m = (xx * 4 + yy) * 2 + cc
        pltpu.make_async_copy(g_all.at[m], g_all.at[m], g3_recv.at[m]).wait()

    gram_ref[...] = g_all[...]

    for cp in c_copies:
        cp.wait_send()
    for i in range(8):
        for k in (1, 2, 3):
            copies_1[i, k].wait_send()
            copies_2[i, k].wait_send()
    for i in range(8):
        @pl.when(4 * (i % 4) + 2 * (i // 4) + c != z)
        def _(i=i):
            z_copy(i, 1)[1].wait_send()

    @pl.when(owner)
    def _():
        @pl.loop(1, 16)
        def _(k):
            zg_copy(k).wait_send()

    @pl.loop(1, 16)
    def _(k):
        for q in range(2):
            pltpu.make_async_copy(pall.at[q], pall.at[q], xy_send.at[k, q]).wait()
        g2_copy(k, z).wait_send()

    pltpu.make_async_copy(theirs, theirs, f_send).wait()

    @pl.loop(1, 32)
    def _(k):
        g1_copy(k).wait_send()
        g3_copy(k).wait_send()


def comm(activations, start_basis):
    dma = pltpu.SemaphoreType.DMA
    return pl.pallas_call(
        comm_kernel,
        out_shape=(jax.ShapeDtypeStruct((K, ROWS), F32), jax.ShapeDtypeStruct((32, 2, K), F32)),
        in_specs=[pl.BlockSpec(memory_space=pl.ANY)] * 2,
        out_specs=(pl.BlockSpec(memory_space=pltpu.VMEM),) * 2,
        scratch_shapes=[
            pltpu.VMEM((16, ROWS, CHUNK), BF16),
            pltpu.VMEM((K, ROWS), BF16),
            pltpu.VMEM((8, 4, 4, 16, 128), F32),
            pltpu.VMEM((8, 4, 4, 16, 128), F32),
            pltpu.VMEM((8, 4, 4, 16, 128), F32),
            pltpu.VMEM((8, 3, 4, 16, 128), F32),
            pltpu.VMEM((8, 4, 16, 128), F32),
            pltpu.VMEM((8, 3, 16, 128), F32),
            pltpu.VMEM((8, 16, 128), F32),
            pltpu.VMEM((16, 16, 128), F32),
            pltpu.VMEM((64, 4, 16, 128), BF16),
            pltpu.VMEM((32, 2, K), F32),
            pltpu.VMEM((32, 2, K), F32),
            pltpu.VMEM((16, 2, K), F32),
            pltpu.VMEM((32, 2, K), F32),
            dma((17,)), dma((8,)), dma((8,)), dma((24,)), dma((24,)), dma((24,)), dma((24,)), dma((8,)), dma((16,)),
            dma((16,)), dma((8,)), dma((16, 2)), dma((16, 2)), dma, dma,
            dma((32,)), dma((32,)), dma((16,)), dma((16,)), dma((32,)), dma((32,)),
        ],
        compiler_params=pltpu.CompilerParams(collective_id=0, has_side_effects=True, vmem_limit_bytes=60 << 20),
        cost_estimate=pl.CostEstimate(flops=4 * ROWS * D * K, bytes_accessed=ROWS * D * 2, transcendentals=0),
        name="reduce_project_gram",
    )(activations, start_basis)


def factor_kernel(gram_ref, img_ref, basis_ref, r_ref):
    g = [gram_ref[8 * i:8 * i + 8, :] for i in range(8)]
    w = [img_ref[8 * i:8 * i + 8, :] for i in range(8)]
    sub = lax.broadcasted_iota(jnp.int32, (8, 128), 0)
    lane = lax.broadcasted_iota(jnp.int32, (8, K), 1)
    row = lax.broadcasted_iota(jnp.int32, (8, K), 0)
    for n in range(8):
        col = [[jnp.broadcast_to(g[i][:, 8 * n + k:8 * n + k + 1], (8, 128)) for i in range(n, 8)] for k in range(8)]
        at = {(h, k): jnp.broadcast_to(col[k][0][h:h + 1, :], (8, 128)) for k in range(8) for h in range(k + 1)}
        scale = jnp.zeros((8, 128), F32)
        for k in range(8):
            inv = 1.0 / at[k, k]
            scale = jnp.where(sub == k, at[k, k], scale)
            m = [c * inv for c in col[k]]
            m[0] = jnp.where(sub > k, m[0], 0.0)
            for k2 in range(k + 1, 8):
                f = at[k, k2] * inv
                for k1 in range(k + 1, k2 + 1):
                    at[k1, k2] = at[k1, k2] - at[k, k1] * f
                for i in range(8 - n):
                    col[k2][i] = col[k2][i] - m[i] * at[k, k2]
            gp = jnp.broadcast_to(g[n][k:k + 1, :], (8, K))
            wp = jnp.broadcast_to(w[n][k:k + 1, :], (8, ROWS))
            for i in range(n, 8):
                g[i] = g[i] - m[i - n][:, :K] * gp
                w[i] = w[i] - jnp.concatenate([m[i - n], m[i - n]], axis=1) * wp
        root = lax.rsqrt(scale)
        r_ref[8 * n:8 * n + 8, :] = jnp.where(lane >= row + 8 * n, g[n] * root[:, :K], 0.0)
        basis_ref[8 * n:8 * n + 8, :] = w[n] * jnp.concatenate([root, root], axis=1)


def factor(gram, image):
    return pl.pallas_call(
        factor_kernel,
        out_shape=(jax.ShapeDtypeStruct((K, ROWS), F32), jax.ShapeDtypeStruct((K, K), F32)),
        name="cholesky_solve",
    )(gram, image)


def on_device(activations, start_basis):
    image, gram = comm(activations, start_basis.T)
    basis, rfactor = factor(gram.reshape(K, K), image)
    return (basis.T, rfactor)


def solution(mesh):
    in_specs = (P(("rows", "grp"), None), P(("rows", "grp"), None))
    out_specs = (P(("rows", "grp"), None), P())
    return jax.shard_map(
        on_device, mesh=mesh, in_specs=in_specs, out_specs=out_specs, check_vma=False
    )
```

```python
import functools
import math

import jax
import jax.numpy as jnp
from jax import lax
from jax.experimental import pallas as pl
from jax.experimental.pallas import tpu as pltpu
from jax.sharding import PartitionSpec as P

MESH = pl.DeviceIdType.MESH
F32 = jnp.float32
BF16 = jnp.bfloat16
ROWS, D, K = 256, 8192, 64
TOTAL = 131072
CHUNK = 512


def comm_kernel(a_hbm, s_hbm, img_ref, gram_ref, a_v, s_v, other, land_c, r1, land_1, r2, land_2, r3, land_z, pall,
                g_own, land_g, g_z, g_all,
                load_sem, c_send, c_recv, s1_send, s1_recv, s2_send, s2_recv, z_send, z_recv,
                zg_send, zg_recv, xy_send, xy_recv, f_send, f_recv,
                g1_send, g1_recv, g2_send, g2_recv, g3_send, g3_recv):
    r = lax.axis_index("rows")
    g = lax.axis_index("grp")
    x, z = r // 16, r % 16
    y, c = g // 2, g % 2

    def dev(xx, yy, zz, cc):
        return (xx * 16 + zz, yy * 2 + cc)

    partner = dev(x, y, z, 1 - c)

    def plane(k):
        return (x + k // 8) % 4, (y + (k // 2) % 4) % 4, (c + k % 2) % 2

    def remote(src, dst, ss, rs, target):
        return pltpu.make_async_remote_copy(src_ref=src, dst_ref=dst, send_sem=ss, recv_sem=rs, device_id=target,
                                            device_id_type=MESH)

    me_a = (x, y)
    me_b = (y, x)
    steps = (2, 1, 3, 0)

    def chunk(half, q, t):
        return (c if half == 0 else 1 - c) * 8 + q * 4 + (me_a[q] + steps[t]) % 4

    def load(half, q, t):
        ch = chunk(half, q, t)
        src = a_hbm.at[:, pl.ds(pl.multiple_of(ch * CHUNK, CHUNK), CHUNK)]
        return pltpu.make_async_copy(src, a_v.at[ch], load_sem.at[(t * 2 + half) * 2 + q])

    load_s = pltpu.make_async_copy(s_hbm, s_v, load_sem.at[16])
    load_s.start()
    for t in range(4):
        for half in (1, 0):
            for q in range(2):
                load(half, q, t).start()

    bar = pltpu.get_barrier_semaphore()
    for k in (8, 7, 9, 6, 10, 5, 11, 4, 12, 3, 13, 2, 14, 1, 15):
        pl.semaphore_signal(bar, inc=1, device_id=dev(x, y, (z + k) % 16, c), device_id_type=MESH)
    for k in range(1, 32):
        xx, yy, cc = plane(k)
        pl.semaphore_signal(bar, inc=1, device_id=dev(xx, yy, z, cc), device_id_type=MESH)

    load_s.wait()
    st = s_v[...]

    def partial(half, q, t, dst):
        part = jnp.dot(st, a_v[chunk(half, q, t)], preferred_element_type=F32)
        for s in range(4):
            for b in range(4):
                dst[q * 4 + s, (me_a[q] + steps[t]) % 4, b] = part[16 * s:16 * s + 16, 128 * b:128 * b + 128]

    def first_peer(q, k):
        return dev((x + k) % 4, y, z, c) if q == 0 else dev(x, (y + k) % 4, z, c)

    def second_peer(q, k):
        return first_peer(1 - q, k)

    def c_copy(q, t):
        a = (me_a[q] + steps[t]) % 4
        four = pl.ds(q * 4, 4)
        return remote(other.at[four, a], land_c.at[four, a], c_send.at[t * 2 + q], c_recv.at[t * 2 + q], partner)

    copies_1 = {}

    def first_axis(t):
        k = steps[t]
        for q in range(2):
            c_copy(q, t).wait_recv()
            a = (me_a[q] + k) % 4
            for s in range(4):
                i = q * 4 + s
                r1[i, a] = r1[i, a] + land_c[i, a]
                if k:
                    n = i * 3 + k - 1
                    copies_1[i, k] = remote(r1.at[i, a], land_1.at[i, k - 1], s1_send.at[n], s1_recv.at[n], first_peer(q, k))
                    copies_1[i, k].start()

    for t in range(4):
        for half in (1, 0):
            for q in range(2):
                load(half, q, t).wait()
        for q in range(2):
            partial(1, q, t, other)
        if t == 0:
            pl.semaphore_wait(bar, 46)
        for q in range(2):
            c_copy(q, t).start()
        for q in range(2):
            partial(0, q, t, r1)
        if t >= 2:
            first_axis(t - 2)
    first_axis(2)
    first_axis(3)

    copies_2 = {}
    for s in range(4):
        for q in range(2):
            i = q * 4 + s
            for k in (1, 2, 3):
                copies_1[i, k].wait_recv()
            r2[i] = (r1[i, me_a[q]] + land_1[i, 0]) + (land_1[i, 1] + land_1[i, 2])
            for k in (1, 2, 3):
                n = i * 3 + k - 1
                cp = remote(r2.at[i, (me_b[q] + k) % 4], land_2.at[i, k - 1], s2_send.at[n], s2_recv.at[n], second_peer(q, k))
                cp.start()
                copies_2[i, k] = cp

    def z_copy(i, slot):
        zo = 4 * (i % 4) + 2 * (i // 4) + c
        return zo, remote(r3.at[i], land_z.at[slot], z_send.at[i], z_recv.at[slot], dev(x, y, zo, c))

    for s in range(4):
        for q in range(2):
            i = q * 4 + s
            for k in (1, 2, 3):
                copies_2[i, k].wait_recv()
            r3[i] = (r2[i, me_b[q]] + land_2[i, 0]) + (land_2[i, 1] + land_2[i, 2])
            zo = 4 * s + 2 * q + c

            @pl.when(zo != z)
            def _(i=i, zo=zo):
                z_copy(i, (zo - z + 16) % 16)[1].start()

    my_s, my_q = z // 4, (z % 4) // 2
    my_i = my_q * 4 + my_s
    owner = z % 2 == c

    def place(q):
        return (c * 2 + q) * 16 + jnp.where(q == 0, x * 4 + y, y * 4 + x)

    def zg_copy(k):
        here = pall.at[place(my_q), my_s]
        return remote(here, here, zg_send.at[k], zg_recv.at[my_i], dev(x, y, (z + k) % 16, c))

    @pl.when(owner)
    def _():
        total = r3[my_i]
        for k in range(1, 16):
            pltpu.make_async_copy(land_z.at[k], land_z.at[k], z_recv.at[k]).wait()
        for k in range(1, 16):
            total = total + land_z[k]
        pall[place(my_q), my_s] = (total * (1.0 / math.sqrt(TOTAL))).astype(BF16)

        for k in (8, 7, 9, 6, 10, 5, 11, 4, 12, 3, 13, 2, 14, 1, 15):
            zg_copy(k).start()

    def xy_copy(k, q, s):
        here = pall.at[place(q), s]
        return remote(here, here, xy_send.at[k, q], xy_recv.at[k, q], dev((x + k // 4) % 4, (y + k % 4) % 4, z, c))

    for j in range(8):
        off = jnp.where(owner, (0, 2, 14, 4, 12, 6, 10, 8)[j], (1, 15, 3, 13, 5, 11, 7, 9)[j])
        zz = (z + off) % 16
        s, q = zz // 4, (zz % 4) // 2

        @pl.when(off != 0)
        def _(s=s, q=q):
            here = pall.at[place(q), s]
            pltpu.make_async_copy(here, here, zg_recv.at[q * 4 + s]).wait()

        for k in range(1, 16):
            xy_copy(k, q, s).start()

    def forward(k, q):
        xx, yy = (x - k // 4 + 4) % 4, (y - k % 4 + 4) % 4
        p = (c * 2 + q) * 16 + (xx * 4 + yy if q == 0 else yy * 4 + xx)
        return p, remote(pall.at[p], pall.at[p], f_send, f_recv, partner)

    for q in range(2):
        forward(0, q)[1].start()

    for k in range(1, 16):
        for q in range(2):
            p, cp = forward(k, q)
            pltpu.make_async_copy(pall.at[p], pall.at[p], xy_recv.at[k, q]).wait()
            cp.start()

    def image_part(half, acc):
        for j in range(8):
            ch = half * 8 + j
            pt = jnp.concatenate([pall[ch * 4 + b].reshape(64, 128) for b in range(4)], axis=1)
            acc = acc + lax.dot_general(pt, a_v[ch], (((1,), (1,)), ((), ())), preferred_element_type=F32)
        return acc

    acc = image_part(c, jnp.zeros((K, ROWS), F32))
    theirs = pall.at[pl.ds((1 - c) * 32, 32)]
    pltpu.make_async_copy(theirs, theirs, f_recv).wait()
    acc = image_part(1 - c, acc)
    img = acc * (1.0 / math.sqrt(D))
    img_ref[...] = img
    gram = lax.dot_general(img, img, (((1,), (1,)), ((), ())), precision=lax.Precision.HIGHEST, preferred_element_type=F32)
    gram = gram * (1.0 / TOTAL)

    for m in range(32):
        g_own[m] = gram[2 * m:2 * m + 2, :]
    me = (x * 4 + y) * 2 + c

    def g1_copy(k):
        xx, yy, cc = plane(k)
        return remote(g_own.at[(xx * 4 + yy) * 2 + cc], land_g.at[k], g1_send, g1_recv, dev(xx, yy, z, cc))

    for k in range(1, 32):
        g1_copy(k).start()

    for t in range(4):
        for q in range(2):
            c_copy(q, t).wait_send()
    for i in range(8):
        for k in (1, 2, 3):
            copies_1[i, k].wait_send()
            copies_2[i, k].wait_send()

        @pl.when(4 * (i % 4) + 2 * (i // 4) + c != z)
        def _(i=i):
            z_copy(i, 1)[1].wait_send()

    @pl.when(owner)
    def _():
        for k in range(1, 16):
            zg_copy(k).wait_send()

    for k in range(1, 16):
        for q in range(2):
            pltpu.make_async_copy(pall.at[q], pall.at[q], xy_send.at[k, q]).wait()
    pltpu.make_async_copy(theirs, theirs, f_send).wait()

    most = land_g.at[pl.ds(1, 31)]
    pltpu.make_async_copy(most, most, g1_recv).wait()
    g_z[z] = g_own[me] + jnp.sum(land_g[1:32], axis=0)

    def g2_copy(k, zs):
        return remote(g_z.at[zs], g_z.at[zs], g2_send.at[k], g2_recv.at[zs], dev(x, y, (z + k) % 16, c))

    for k in (8, 7, 9, 6, 10, 5, 11, 4, 12, 3, 13, 2, 14, 1, 15):
        g2_copy(k, z).start()
    pltpu.make_async_copy(most, most, g1_send).wait()
    for k in range(1, 16):
        g2_copy(k, (z + k) % 16).wait_recv()
    g_all[me] = jnp.sum(g_z[...], axis=0)

    def g3_copy(k):
        xx, yy, cc = plane(k)
        return remote(g_all.at[me], g_all.at[me], g3_send, g3_recv, dev(xx, yy, z, cc))

    for k in range(1, 32):
        g3_copy(k).start()
    for k in range(1, 16):
        g2_copy(k, z).wait_send()
    others = g_all.at[pl.ds(0, 31)]
    pltpu.make_async_copy(others, others, g3_recv).wait()
    gram_ref[...] = g_all[...]
    pltpu.make_async_copy(others, others, g3_send).wait()


def comm(activations, start_basis):
    dma = pltpu.SemaphoreType.DMA
    return pl.pallas_call(
        comm_kernel,
        out_shape=(jax.ShapeDtypeStruct((K, ROWS), F32), jax.ShapeDtypeStruct((32, 2, K), F32)),
        in_specs=[pl.BlockSpec(memory_space=pl.ANY)] * 2,
        out_specs=(pl.BlockSpec(memory_space=pltpu.VMEM),) * 2,
        scratch_shapes=[
            pltpu.VMEM((16, ROWS, CHUNK), BF16),
            pltpu.VMEM((K, ROWS), BF16),
            pltpu.VMEM((8, 4, 4, 16, 128), F32),
            pltpu.VMEM((8, 4, 4, 16, 128), F32),
            pltpu.VMEM((8, 4, 4, 16, 128), F32),
            pltpu.VMEM((8, 3, 4, 16, 128), F32),
            pltpu.VMEM((8, 4, 16, 128), F32),
            pltpu.VMEM((8, 3, 16, 128), F32),
            pltpu.VMEM((8, 16, 128), F32),
            pltpu.VMEM((16, 16, 128), F32),
            pltpu.VMEM((64, 4, 16, 128), BF16),
            pltpu.VMEM((32, 2, K), F32),
            pltpu.VMEM((32, 2, K), F32),
            pltpu.VMEM((16, 2, K), F32),
            pltpu.VMEM((32, 2, K), F32),
            dma((17,)), dma((8,)), dma((8,)), dma((24,)), dma((24,)), dma((24,)), dma((24,)), dma((8,)), dma((16,)),
            dma((16,)), dma((8,)), dma((16, 2)), dma((16, 2)), dma, dma,
            dma, dma, dma((16,)), dma((16,)), dma, dma,
        ],
        compiler_params=pltpu.CompilerParams(collective_id=0, has_side_effects=True, vmem_limit_bytes=60 << 20),
        cost_estimate=pl.CostEstimate(flops=4 * ROWS * D * K, bytes_accessed=ROWS * D * 2, transcendentals=0),
        name="reduce_project_gram",
    )(activations, start_basis)


def factor_kernel(gram_ref, img_ref, basis_ref, r_ref):
    g = [gram_ref[8 * i:8 * i + 8, :] for i in range(8)]
    w = [img_ref[8 * i:8 * i + 8, :] for i in range(8)]
    sub = lax.broadcasted_iota(jnp.int32, (8, 128), 0)
    lane = lax.broadcasted_iota(jnp.int32, (8, K), 1)
    row = lax.broadcasted_iota(jnp.int32, (8, K), 0)
    for n in range(8):
        col = [[jnp.broadcast_to(g[i][:, 8 * n + k:8 * n + k + 1], (8, 128)) for i in range(n, 8)] for k in range(8)]
        at = {(h, k): jnp.broadcast_to(col[k][0][h:h + 1, :], (8, 128)) for k in range(8) for h in range(k + 1)}
        scale = jnp.zeros((8, 128), F32)
        for k in range(8):
            inv = 1.0 / at[k, k]
            scale = jnp.where(sub == k, at[k, k], scale)
            m = [c * inv for c in col[k]]
            m[0] = jnp.where(sub > k, m[0], 0.0)
            for k2 in range(k + 1, 8):
                f = at[k, k2] * inv
                for k1 in range(k + 1, k2 + 1):
                    at[k1, k2] = at[k1, k2] - at[k, k1] * f
                for i in range(8 - n):
                    col[k2][i] = col[k2][i] - m[i] * at[k, k2]
            gp = jnp.broadcast_to(g[n][k:k + 1, :], (8, K))
            wp = jnp.broadcast_to(w[n][k:k + 1, :], (8, ROWS))
            for i in range(n, 8):
                g[i] = g[i] - m[i - n][:, :K] * gp
                w[i] = w[i] - jnp.concatenate([m[i - n], m[i - n]], axis=1) * wp
        root = lax.rsqrt(scale)
        r_ref[8 * n:8 * n + 8, :] = jnp.where(lane >= row + 8 * n, g[n] * root[:, :K], 0.0)
        basis_ref[8 * n:8 * n + 8, :] = w[n] * jnp.concatenate([root, root], axis=1)


def factor(gram, image):
    return pl.pallas_call(
        factor_kernel,
        out_shape=(jax.ShapeDtypeStruct((K, ROWS), F32), jax.ShapeDtypeStruct((K, K), F32)),
        name="cholesky_solve",
    )(gram, image)


def on_device(activations, start_basis):
    image, gram = comm(activations, start_basis.T)
    basis, rfactor = factor(gram.reshape(K, K), image)
    return (basis.T, rfactor)


def solution(mesh):
    in_specs = (P(("rows", "grp"), None), P(("rows", "grp"), None))
    out_specs = (P(("rows", "grp"), None), P())
    return jax.shard_map(
        on_device, mesh=mesh, in_specs=in_specs, out_specs=out_specs, check_vma=False
    )
```

```python
import functools
import math

import jax
import jax.numpy as jnp
from jax import lax
from jax.experimental import pallas as pl
from jax.experimental.pallas import tpu as pltpu
from jax.sharding import PartitionSpec as P

MESH = pl.DeviceIdType.MESH
F32 = jnp.float32
BF16 = jnp.bfloat16
ROWS, D, K = 256, 8192, 64
TOTAL = 131072
CHUNK = 512


def comm_kernel(a_hbm, s_hbm, img_ref, gram_ref, a_v, s_v, other, land_c, r1, land_1, r2, land_2, r3, land_z, pall,
                g_own, land_g, g_z, g_all,
                load_sem, c_send, c_recv, s1_send, s1_recv, s2_send, s2_recv, z_send, z_recv,
                zg_send, zg_recv, xy_send, xy_recv, f_send, f_recv,
                g1_send, g1_recv, g2_send, g2_recv, g3_send, g3_recv, know):
    r = lax.axis_index("rows")
    g = lax.axis_index("grp")
    x, z = r // 16, r % 16
    y, c = g // 2, g % 2

    def dev(xx, yy, zz, cc):
        return (xx * 16 + zz, yy * 2 + cc)

    partner = dev(x, y, z, 1 - c)

    def plane(k):
        return (x + k // 8) % 4, (y + (k // 2) % 4) % 4, (c + k % 2) % 2

    def remote(src, dst, ss, rs, target):
        return pltpu.make_async_remote_copy(src_ref=src, dst_ref=dst, send_sem=ss, recv_sem=rs, device_id=target,
                                            device_id_type=MESH)

    me_a = (x, y)
    me_b = (y, x)
    steps = (2, 1, 3, 0)

    def chunk(half, q, t):
        return (c if half == 0 else 1 - c) * 8 + q * 4 + (me_a[q] + steps[t]) % 4

    def load(half, q, t):
        ch = chunk(half, q, t)
        src = a_hbm.at[:, pl.ds(pl.multiple_of(ch * CHUNK, CHUNK), CHUNK)]
        return pltpu.make_async_copy(src, a_v.at[ch], load_sem.at[(t * 2 + half) * 2 + q])

    bar = pltpu.get_barrier_semaphore()
    x_peers = [dev((x + k) % 4, y, z, c) for k in (1, 2, 3)]
    y_peers = [dev(x, (y + k) % 4, z, c) for k in (1, 2, 3)]

    def z_peers(k):
        return [dev(x, y, (z + k) % 16, c), dev(x, y, (z + 16 - k) % 16, c)]

    def greet(sem, targets):
        for target in targets:
            pl.semaphore_signal(sem, inc=1, device_id=target, device_id_type=MESH)

    greet(bar, [partner] + x_peers + y_peers + z_peers(1))

    load_s = pltpu.make_async_copy(s_hbm, s_v, load_sem.at[16])
    load_s.start()
    for t in range(4):
        for half in (1, 0):
            for q in range(2):
                load(half, q, t).start()

    load_s.wait()
    st = s_v[...]

    def partial(half, q, t, dst):
        part = jnp.dot(st, a_v[chunk(half, q, t)], preferred_element_type=F32)
        for s in range(4):
            for b in range(4):
                dst[q * 4 + s, (me_a[q] + steps[t]) % 4, b] = part[16 * s:16 * s + 16, 128 * b:128 * b + 128]

    def first_peer(q, k):
        return dev((x + k) % 4, y, z, c) if q == 0 else dev(x, (y + k) % 4, z, c)

    def second_peer(q, k):
        return first_peer(1 - q, k)

    def c_copy(q, t):
        a = (me_a[q] + steps[t]) % 4
        four = pl.ds(q * 4, 4)
        return remote(other.at[four, a], land_c.at[four, a], c_send.at[t * 2 + q], c_recv.at[t * 2 + q], partner)

    copies_1 = {}

    def first_axis(t):
        k = steps[t]
        for q in range(2):
            c_copy(q, t).wait_recv()
            a = (me_a[q] + k) % 4
            for s in range(4):
                i = q * 4 + s
                r1[i, a] = r1[i, a] + land_c[i, a]
                if k:
                    n = i * 3 + k - 1
                    copies_1[i, k] = remote(r1.at[i, a], land_1.at[i, k - 1], s1_send.at[n], s1_recv.at[n], first_peer(q, k))
                    copies_1[i, k].start()

    for t in range(4):
        for half in (1, 0):
            for q in range(2):
                load(half, q, t).wait()
        for q in range(2):
            partial(1, q, t, other)
        if t == 0:
            pl.semaphore_wait(bar, 9)
        for q in range(2):
            c_copy(q, t).start()
        if t == 0:
            greet(know.at[0], y_peers)
            greet(know.at[1], z_peers(1))
        for q in range(2):
            partial(0, q, t, r1)
        if t >= 2:
            first_axis(t - 2)
    first_axis(2)
    first_axis(3)
    pl.semaphore_wait(know.at[0], 3)
    greet(know.at[2], [partner])
    pl.semaphore_wait(know.at[1], 2)
    greet(know.at[3], z_peers(2))

    copies_2 = {}
    for s in range(4):
        for q in range(2):
            i = q * 4 + s
            for k in (1, 2, 3):
                copies_1[i, k].wait_recv()
            r2[i] = (r1[i, me_a[q]] + land_1[i, 0]) + (land_1[i, 1] + land_1[i, 2])
            for k in (1, 2, 3):
                n = i * 3 + k - 1
                cp = remote(r2.at[i, (me_b[q] + k) % 4], land_2.at[i, k - 1], s2_send.at[n], s2_recv.at[n], second_peer(q, k))
                cp.start()
                copies_2[i, k] = cp

    pl.semaphore_wait(know.at[3], 2)
    greet(know.at[4], z_peers(4))

    def z_copy(i, slot):
        zo = 4 * (i % 4) + 2 * (i // 4) + c
        return zo, remote(r3.at[i], land_z.at[slot], z_send.at[i], z_recv.at[slot], dev(x, y, zo, c))

    for s in range(4):
        for q in range(2):
            i = q * 4 + s
            for k in (1, 2, 3):
                copies_2[i, k].wait_recv()
            r3[i] = (r2[i, me_b[q]] + land_2[i, 0]) + (land_2[i, 1] + land_2[i, 2])
            if i == 0:
                pl.semaphore_wait(know.at[4], 2)
            zo = 4 * s + 2 * q + c

            @pl.when(zo != z)
            def _(i=i, zo=zo):
                z_copy(i, (zo - z + 16) % 16)[1].start()

    my_s, my_q = z // 4, (z % 4) // 2
    my_i = my_q * 4 + my_s
    owner = z % 2 == c

    def place(q):
        return (c * 2 + q) * 16 + jnp.where(q == 0, x * 4 + y, y * 4 + x)

    def zg_copy(k):
        here = pall.at[place(my_q), my_s]
        return remote(here, here, zg_send.at[k], zg_recv.at[my_i], dev(x, y, (z + k) % 16, c))

    @pl.when(owner)
    def _():
        total = r3[my_i]
        for k in range(1, 16):
            pltpu.make_async_copy(land_z.at[k], land_z.at[k], z_recv.at[k]).wait()
        for k in range(1, 16):
            total = total + land_z[k]
        pall[place(my_q), my_s] = (total * (1.0 / math.sqrt(TOTAL))).astype(BF16)

        for k in (8, 7, 9, 6, 10, 5, 11, 4, 12, 3, 13, 2, 14, 1, 15):
            zg_copy(k).start()

    def xy_copy(k, q, s):
        here = pall.at[place(q), s]
        return remote(here, here, xy_send.at[k, q], xy_recv.at[k, q], dev((x + k // 4) % 4, (y + k % 4) % 4, z, c))

    for j in range(8):
        off = jnp.where(owner, (0, 2, 14, 4, 12, 6, 10, 8)[j], (1, 15, 3, 13, 5, 11, 7, 9)[j])
        zz = (z + off) % 16
        s, q = zz // 4, (zz % 4) // 2

        @pl.when(off != 0)
        def _(s=s, q=q):
            here = pall.at[place(q), s]
            pltpu.make_async_copy(here, here, zg_recv.at[q * 4 + s]).wait()

        for k in range(1, 16):
            xy_copy(k, q, s).start()

    def forward(k, q):
        xx, yy = (x - k // 4 + 4) % 4, (y - k % 4 + 4) % 4
        p = (c * 2 + q) * 16 + (xx * 4 + yy if q == 0 else yy * 4 + xx)
        return p, remote(pall.at[p], pall.at[p], f_send, f_recv, partner)

    for q in range(2):
        forward(0, q)[1].start()

    for k in range(1, 16):
        for q in range(2):
            p, cp = forward(k, q)
            pltpu.make_async_copy(pall.at[p], pall.at[p], xy_recv.at[k, q]).wait()
            cp.start()

    def image_part(half, acc):
        for j in range(8):
            ch = half * 8 + j
            pt = jnp.concatenate([pall[ch * 4 + b].reshape(64, 128) for b in range(4)], axis=1)
            acc = acc + lax.dot_general(pt, a_v[ch], (((1,), (1,)), ((), ())), preferred_element_type=F32)
        return acc

    acc = image_part(c, jnp.zeros((K, ROWS), F32))
    theirs = pall.at[pl.ds((1 - c) * 32, 32)]
    pltpu.make_async_copy(theirs, theirs, f_recv).wait()
    acc = image_part(1 - c, acc)
    img = acc * (1.0 / math.sqrt(D))
    img_ref[...] = img
    gram = lax.dot_general(img, img, (((1,), (1,)), ((), ())), precision=lax.Precision.HIGHEST, preferred_element_type=F32)
    gram = gram * (1.0 / TOTAL)

    for m in range(32):
        g_own[m] = gram[2 * m:2 * m + 2, :]
    me = (x * 4 + y) * 2 + c

    def g1_copy(k):
        xx, yy, cc = plane(k)
        return remote(g_own.at[(xx * 4 + yy) * 2 + cc], land_g.at[k], g1_send, g1_recv, dev(xx, yy, z, cc))

    pl.semaphore_wait(know.at[2], 1)
    for k in range(1, 32):
        g1_copy(k).start()

    for t in range(4):
        for q in range(2):
            c_copy(q, t).wait_send()
    for i in range(8):
        for k in (1, 2, 3):
            copies_1[i, k].wait_send()
            copies_2[i, k].wait_send()

        @pl.when(4 * (i % 4) + 2 * (i // 4) + c != z)
        def _(i=i):
            z_copy(i, 1)[1].wait_send()

    @pl.when(owner)
    def _():
        for k in range(1, 16):
            zg_copy(k).wait_send()

    for k in range(1, 16):
        for q in range(2):
            pltpu.make_async_copy(pall.at[q], pall.at[q], xy_send.at[k, q]).wait()
    pltpu.make_async_copy(theirs, theirs, f_send).wait()

    most = land_g.at[pl.ds(1, 31)]
    pltpu.make_async_copy(most, most, g1_recv).wait()
    g_z[z] = g_own[me] + jnp.sum(land_g[1:32], axis=0)

    def g2_copy(k, zs):
        return remote(g_z.at[zs], g_z.at[zs], g2_send.at[k], g2_recv.at[zs], dev(x, y, (z + k) % 16, c))

    for k in (8, 7, 9, 6, 10, 5, 11, 4, 12, 3, 13, 2, 14, 1, 15):
        g2_copy(k, z).start()
    pltpu.make_async_copy(most, most, g1_send).wait()
    for k in range(1, 16):
        g2_copy(k, (z + k) % 16).wait_recv()
    g_all[me] = jnp.sum(g_z[...], axis=0)

    def g3_copy(k):
        xx, yy, cc = plane(k)
        return remote(g_all.at[me], g_all.at[me], g3_send, g3_recv, dev(xx, yy, z, cc))

    for k in range(1, 32):
        g3_copy(k).start()
    for k in range(1, 16):
        g2_copy(k, z).wait_send()
    others = g_all.at[pl.ds(0, 31)]
    pltpu.make_async_copy(others, others, g3_recv).wait()
    gram_ref[...] = g_all[...]
    pltpu.make_async_copy(others, others, g3_send).wait()


def comm(activations, start_basis):
    dma = pltpu.SemaphoreType.DMA
    return pl.pallas_call(
        comm_kernel,
        out_shape=(jax.ShapeDtypeStruct((K, ROWS), F32), jax.ShapeDtypeStruct((32, 2, K), F32)),
        in_specs=[pl.BlockSpec(memory_space=pl.ANY)] * 2,
        out_specs=(pl.BlockSpec(memory_space=pltpu.VMEM),) * 2,
        scratch_shapes=[
            pltpu.VMEM((16, ROWS, CHUNK), BF16),
            pltpu.VMEM((K, ROWS), BF16),
            pltpu.VMEM((8, 4, 4, 16, 128), F32),
            pltpu.VMEM((8, 4, 4, 16, 128), F32),
            pltpu.VMEM((8, 4, 4, 16, 128), F32),
            pltpu.VMEM((8, 3, 4, 16, 128), F32),
            pltpu.VMEM((8, 4, 16, 128), F32),
            pltpu.VMEM((8, 3, 16, 128), F32),
            pltpu.VMEM((8, 16, 128), F32),
            pltpu.VMEM((16, 16, 128), F32),
            pltpu.VMEM((64, 4, 16, 128), BF16),
            pltpu.VMEM((32, 2, K), F32),
            pltpu.VMEM((32, 2, K), F32),
            pltpu.VMEM((16, 2, K), F32),
            pltpu.VMEM((32, 2, K), F32),
            dma((17,)), dma((8,)), dma((8,)), dma((24,)), dma((24,)), dma((24,)), dma((24,)), dma((8,)), dma((16,)),
            dma((16,)), dma((8,)), dma((16, 2)), dma((16, 2)), dma, dma,
            dma, dma, dma((16,)), dma((16,)), dma, dma, pltpu.SemaphoreType.REGULAR((5,)),
        ],
        compiler_params=pltpu.CompilerParams(collective_id=0, has_side_effects=True, vmem_limit_bytes=60 << 20),
        cost_estimate=pl.CostEstimate(flops=4 * ROWS * D * K, bytes_accessed=ROWS * D * 2, transcendentals=0),
        name="reduce_project_gram",
    )(activations, start_basis)


def factor_kernel(gram_ref, img_ref, basis_ref, r_ref):
    g = [gram_ref[8 * i:8 * i + 8, :] for i in range(8)]
    w = [img_ref[8 * i:8 * i + 8, :] for i in range(8)]
    sub = lax.broadcasted_iota(jnp.int32, (8, 128), 0)
    lane = lax.broadcasted_iota(jnp.int32, (8, K), 1)
    row = lax.broadcasted_iota(jnp.int32, (8, K), 0)
    for n in range(8):
        col = [[jnp.broadcast_to(g[i][:, 8 * n + k:8 * n + k + 1], (8, 128)) for i in range(n, 8)] for k in range(8)]
        at = {(h, k): jnp.broadcast_to(col[k][0][h:h + 1, :], (8, 128)) for k in range(8) for h in range(k + 1)}
        scale = jnp.zeros((8, 128), F32)
        for k in range(8):
            inv = 1.0 / at[k, k]
            scale = jnp.where(sub == k, at[k, k], scale)
            m = [c * inv for c in col[k]]
            m[0] = jnp.where(sub > k, m[0], 0.0)
            for k2 in range(k + 1, 8):
                f = at[k, k2] * inv
                for k1 in range(k + 1, k2 + 1):
                    at[k1, k2] = at[k1, k2] - at[k, k1] * f
                for i in range(8 - n):
                    col[k2][i] = col[k2][i] - m[i] * at[k, k2]
            gp = jnp.broadcast_to(g[n][k:k + 1, :], (8, K))
            wp = jnp.broadcast_to(w[n][k:k + 1, :], (8, ROWS))
            for i in range(n, 8):
                g[i] = g[i] - m[i - n][:, :K] * gp
                w[i] = w[i] - jnp.concatenate([m[i - n], m[i - n]], axis=1) * wp
        root = lax.rsqrt(scale)
        r_ref[8 * n:8 * n + 8, :] = jnp.where(lane >= row + 8 * n, g[n] * root[:, :K], 0.0)
        basis_ref[8 * n:8 * n + 8, :] = w[n] * jnp.concatenate([root, root], axis=1)


def factor(gram, image):
    return pl.pallas_call(
        factor_kernel,
        out_shape=(jax.ShapeDtypeStruct((K, ROWS), F32), jax.ShapeDtypeStruct((K, K), F32)),
        name="cholesky_solve",
    )(gram, image)


def on_device(activations, start_basis):
    image, gram = comm(activations, start_basis.T)
    basis, rfactor = factor(gram.reshape(K, K), image)
    return (basis.T, rfactor)


def solution(mesh):
    in_specs = (P(("rows", "grp"), None), P(("rows", "grp"), None))
    out_specs = (P(("rows", "grp"), None), P())
    return jax.shard_map(
        on_device, mesh=mesh, in_specs=in_specs, out_specs=out_specs, check_vma=False
    )
```

```python
import functools
import math

import jax
import jax.numpy as jnp
from jax import lax
from jax.experimental import pallas as pl
from jax.experimental.pallas import tpu as pltpu
from jax.sharding import PartitionSpec as P

MESH = pl.DeviceIdType.MESH
F32 = jnp.float32
BF16 = jnp.bfloat16
ROWS, D, K = 256, 8192, 64
TOTAL = 131072
CHUNK = 512


def comm_kernel(a_hbm, s_hbm, img_ref, gram_ref, a_v, s_v, other, land_c, r1, land_1, r2, land_2, r3, land_z, pall,
                g_own, land_g, g_z, g_all,
                load_sem, c_send, c_recv, s1_send, s1_recv, s2_send, s2_recv, z_send, z_recv,
                zg_send, zg_recv, xy_send, xy_recv, f_send, f_recv,
                g1_send, g1_recv, g2_send, g2_recv, g3_send, g3_recv, know):
    r = lax.axis_index("rows")
    g = lax.axis_index("grp")
    x, z = r // 16, r % 16
    y, c = g // 2, g % 2

    def dev(xx, yy, zz, cc):
        return (xx * 16 + zz, yy * 2 + cc)

    partner = dev(x, y, z, 1 - c)

    def plane(k):
        return (x + k // 8) % 4, (y + (k // 2) % 4) % 4, (c + k % 2) % 2

    def remote(src, dst, ss, rs, target):
        return pltpu.make_async_remote_copy(src_ref=src, dst_ref=dst, send_sem=ss, recv_sem=rs, device_id=target,
                                            device_id_type=MESH)

    def arrived(ref, sem):
        pltpu.make_async_copy(ref, ref, sem).wait()

    me_a = (x, y)
    me_b = (y, x)
    steps = (2, 1, 3, 0)

    def chunk(half, q, t):
        return (c if half == 0 else 1 - c) * 8 + q * 4 + (me_a[q] + steps[t]) % 4

    def load(half, q, t):
        ch = chunk(half, q, t)
        src = a_hbm.at[:, pl.ds(pl.multiple_of(ch * CHUNK, CHUNK), CHUNK)]
        return pltpu.make_async_copy(src, a_v.at[ch], load_sem.at[t])

    bar = pltpu.get_barrier_semaphore()
    x_peers = [dev((x + k) % 4, y, z, c) for k in (1, 2, 3)]
    y_peers = [dev(x, (y + k) % 4, z, c) for k in (1, 2, 3)]

    def z_peers(k):
        return [dev(x, y, (z + k) % 16, c), dev(x, y, (z + 16 - k) % 16, c)]

    def greet(sem, targets):
        for target in targets:
            pl.semaphore_signal(sem, inc=1, device_id=target, device_id_type=MESH)

    greet(bar, [partner] + x_peers + y_peers + z_peers(1))

    load_s = pltpu.make_async_copy(s_hbm, s_v, load_sem.at[4])
    load_s.start()
    for t in range(4):
        for half in (1, 0):
            for q in range(2):
                load(half, q, t).start()

    load_s.wait()
    st = s_v[...]

    def partial(half, q, t, dst):
        part = jnp.dot(st, a_v[chunk(half, q, t)], preferred_element_type=F32)
        for s in range(4):
            for b in range(4):
                dst[q * 4 + s, (me_a[q] + steps[t]) % 4, b] = part[16 * s:16 * s + 16, 128 * b:128 * b + 128]

    def first_peer(q, k):
        return dev((x + k) % 4, y, z, c) if q == 0 else dev(x, (y + k) % 4, z, c)

    def second_peer(q, k):
        return first_peer(1 - q, k)

    def c_copy(q, t):
        a = (me_a[q] + steps[t]) % 4
        four = pl.ds(q * 4, 4)
        return remote(other.at[four, a], land_c.at[four, a], c_send, c_recv.at[t], partner)

    def first_axis(t):
        k = steps[t]
        arrived(land_c.at[pl.ds(0, 2)], c_recv.at[t])
        for q in range(2):
            a = (me_a[q] + k) % 4
            for s in range(4):
                i = q * 4 + s
                r1[i, a] = r1[i, a] + land_c[i, a]
                if k:
                    remote(r1.at[i, a], land_1.at[i, k - 1], s1_send, s1_recv.at[s], first_peer(q, k)).start()

    for t in range(4):
        arrived(a_v.at[pl.ds(0, 4)], load_sem.at[t])
        for q in range(2):
            partial(1, q, t, other)
        for q in range(2):
            partial(0, q, t, r1)
        if t == 0:
            pl.semaphore_wait(bar, 9)
        for q in range(2):
            c_copy(q, t).start()
        if t == 0:
            greet(know.at[0], y_peers)
            greet(know.at[1], z_peers(1))
        if t >= 1:
            first_axis(t - 1)
    first_axis(3)
    pl.semaphore_wait(know.at[0], 3)
    greet(know.at[2], [partner])
    pl.semaphore_wait(know.at[1], 2)
    greet(know.at[3], z_peers(2))
    pl.semaphore_wait(know.at[3], 2)
    greet(know.at[4], z_peers(4))

    for s in range(4):
        arrived(land_1.at[pl.ds(0, 2)], s1_recv.at[s])
        for q in range(2):
            i = q * 4 + s
            r2[i] = (r1[i, me_a[q]] + land_1[i, 0]) + (land_1[i, 1] + land_1[i, 2])
            for k in (1, 2, 3):
                remote(r2.at[i, (me_b[q] + k) % 4], land_2.at[i, k - 1], s2_send, s2_recv.at[s], second_peer(q, k)).start()

    def z_copy(i, slot):
        zo = 4 * (i % 4) + 2 * (i // 4) + c
        return zo, remote(r3.at[i], land_z.at[slot], z_send, z_recv, dev(x, y, zo, c))

    for s in range(4):
        arrived(land_2.at[pl.ds(0, 2)], s2_recv.at[s])
        for q in range(2):
            i = q * 4 + s
            r3[i] = (r2[i, me_b[q]] + land_2[i, 0]) + (land_2[i, 1] + land_2[i, 2])
            if i == 0:
                pl.semaphore_wait(know.at[4], 2)
            zo = 4 * s + 2 * q + c

            @pl.when(zo != z)
            def _(i=i, zo=zo):
                z_copy(i, (zo - z + 16) % 16)[1].start()

    my_s, my_q = z // 4, (z % 4) // 2
    my_i = my_q * 4 + my_s
    owner = z % 2 == c

    def place(q):
        return (c * 2 + q) * 16 + jnp.where(q == 0, x * 4 + y, y * 4 + x)

    def zg_copy(k):
        here = pall.at[place(my_q), my_s]
        return remote(here, here, zg_send, zg_recv.at[my_i], dev(x, y, (z + k) % 16, c))

    @pl.when(owner)
    def _():
        total = r3[my_i]
        arrived(land_z.at[pl.ds(1, 15)], z_recv)
        for k in range(1, 16):
            total = total + land_z[k]
        pall[place(my_q), my_s] = (total * (1.0 / math.sqrt(TOTAL))).astype(BF16)

        for k in (8, 7, 9, 6, 10, 5, 11, 4, 12, 3, 13, 2, 14, 1, 15):
            zg_copy(k).start()

    def far(k):
        return min(k // 4, 4 - k // 4) + min(k % 4, 4 - k % 4)

    def xy_copy(k, q, s):
        here = pall.at[place(q), s]
        return remote(here, here, xy_send, xy_recv.at[far(k) - 1], dev((x + k // 4) % 4, (y + k % 4) % 4, z, c))

    for j in range(8):
        off = jnp.where(owner, (0, 2, 14, 4, 12, 6, 10, 8)[j], (1, 15, 3, 13, 5, 11, 7, 9)[j])
        zz = (z + off) % 16
        s, q = zz // 4, (zz % 4) // 2

        @pl.when(off != 0)
        def _(s=s, q=q):
            arrived(pall.at[place(q), s], zg_recv.at[q * 4 + s])

        for k in range(1, 16):
            xy_copy(k, q, s).start()

    def forward(k, q):
        xx, yy = (x - k // 4 + 4) % 4, (y - k % 4 + 4) % 4
        p = (c * 2 + q) * 16 + (xx * 4 + yy if q == 0 else yy * 4 + xx)
        return remote(pall.at[p], pall.at[p], f_send, f_recv, partner)

    for q in range(2):
        forward(0, q).start()

    for hops in range(1, 5):
        ring = [k for k in range(1, 16) if far(k) == hops]
        arrived(pall.at[pl.ds(0, 2 * len(ring))], xy_recv.at[hops - 1])
        for k in ring:
            for q in range(2):
                forward(k, q).start()

    def image_part(half, acc):
        for j in range(8):
            ch = half * 8 + j
            pt = jnp.concatenate([pall[ch * 4 + b].reshape(64, 128) for b in range(4)], axis=1)
            acc = acc + lax.dot_general(pt, a_v[ch], (((1,), (1,)), ((), ())), preferred_element_type=F32)
        return acc

    acc = image_part(c, jnp.zeros((K, ROWS), F32))
    theirs = pall.at[pl.ds((1 - c) * 32, 32)]
    arrived(theirs, f_recv)
    acc = image_part(1 - c, acc)
    img = acc * (1.0 / math.sqrt(D))
    img_ref[...] = img
    gram = lax.dot_general(img, img, (((1,), (1,)), ((), ())), precision=lax.Precision.HIGHEST, preferred_element_type=F32)
    gram = gram * (1.0 / TOTAL)

    for m in range(32):
        g_own[m] = gram[2 * m:2 * m + 2, :]
    me = (x * 4 + y) * 2 + c

    def g1_copy(k):
        xx, yy, cc = plane(k)
        return remote(g_own.at[(xx * 4 + yy) * 2 + cc], land_g.at[k], g1_send, g1_recv, dev(xx, yy, z, cc))

    pl.semaphore_wait(know.at[2], 1)
    for k in range(1, 32):
        g1_copy(k).start()

    arrived(other, c_send)
    arrived(r1.at[pl.ds(0, 6)], s1_send)
    arrived(r2.at[pl.ds(0, 6)], s2_send)

    @pl.when(owner)
    def _():
        arrived(r3.at[pl.ds(0, 7)], z_send)
        arrived(land_z.at[pl.ds(0, 15), pl.ds(0, 8)], zg_send)

    @pl.when(jnp.logical_not(owner))
    def _():
        arrived(r3, z_send)

    arrived(pall.at[pl.ds(0, 30)], xy_send)
    arrived(theirs, f_send)

    most = land_g.at[pl.ds(1, 31)]
    arrived(most, g1_recv)
    g_z[z] = g_own[me] + jnp.sum(land_g[1:32], axis=0)

    def g2_copy(k):
        return remote(g_z.at[z], g_z.at[z], g2_send, g2_recv, dev(x, y, (z + k) % 16, c))

    for k in (8, 7, 9, 6, 10, 5, 11, 4, 12, 3, 13, 2, 14, 1, 15):
        g2_copy(k).start()
    arrived(most, g1_send)
    line = g_z.at[pl.ds(0, 15)]
    arrived(line, g2_recv)
    g_all[me] = jnp.sum(g_z[...], axis=0)

    def g3_copy(k):
        xx, yy, cc = plane(k)
        return remote(g_all.at[me], g_all.at[me], g3_send, g3_recv, dev(xx, yy, z, cc))

    for k in range(1, 32):
        g3_copy(k).start()
    arrived(line, g2_send)
    others = g_all.at[pl.ds(0, 31)]
    arrived(others, g3_recv)
    gram_ref[...] = g_all[...]
    arrived(others, g3_send)


def comm(activations, start_basis):
    dma = pltpu.SemaphoreType.DMA
    return pl.pallas_call(
        comm_kernel,
        out_shape=(jax.ShapeDtypeStruct((K, ROWS), F32), jax.ShapeDtypeStruct((32, 2, K), F32)),
        in_specs=[pl.BlockSpec(memory_space=pl.ANY)] * 2,
        out_specs=(pl.BlockSpec(memory_space=pltpu.VMEM),) * 2,
        scratch_shapes=[
            pltpu.VMEM((16, ROWS, CHUNK), BF16),
            pltpu.VMEM((K, ROWS), BF16),
            pltpu.VMEM((8, 4, 4, 16, 128), F32),
            pltpu.VMEM((8, 4, 4, 16, 128), F32),
            pltpu.VMEM((8, 4, 4, 16, 128), F32),
            pltpu.VMEM((8, 3, 4, 16, 128), F32),
            pltpu.VMEM((8, 4, 16, 128), F32),
            pltpu.VMEM((8, 3, 16, 128), F32),
            pltpu.VMEM((8, 16, 128), F32),
            pltpu.VMEM((16, 16, 128), F32),
            pltpu.VMEM((64, 4, 16, 128), BF16),
            pltpu.VMEM((32, 2, K), F32),
            pltpu.VMEM((32, 2, K), F32),
            pltpu.VMEM((16, 2, K), F32),
            pltpu.VMEM((32, 2, K), F32),
            dma((5,)), dma, dma((4,)), dma, dma((4,)), dma, dma((4,)), dma, dma,
            dma, dma((8,)), dma, dma((4,)), dma, dma,
            dma, dma, dma, dma, dma, dma, pltpu.SemaphoreType.REGULAR((5,)),
        ],
        compiler_params=pltpu.CompilerParams(collective_id=0, has_side_effects=True, vmem_limit_bytes=60 << 20),
        cost_estimate=pl.CostEstimate(flops=4 * ROWS * D * K, bytes_accessed=ROWS * D * 2, transcendentals=0),
        name="reduce_project_gram",
    )(activations, start_basis)


def factor_kernel(gram_ref, img_ref, basis_ref, r_ref):
    g = [gram_ref[8 * i:8 * i + 8, :] for i in range(8)]
    w = [img_ref[8 * i:8 * i + 8, :] for i in range(8)]
    sub = lax.broadcasted_iota(jnp.int32, (8, 128), 0)
    lane = lax.broadcasted_iota(jnp.int32, (8, K), 1)
    row = lax.broadcasted_iota(jnp.int32, (8, K), 0)
    for n in range(8):
        col = [[jnp.broadcast_to(g[i][:, 8 * n + k:8 * n + k + 1], (8, 128)) for i in range(n, 8)] for k in range(8)]
        at = {(h, k): jnp.broadcast_to(col[k][0][h:h + 1, :], (8, 128)) for k in range(8) for h in range(k + 1)}
        scale = jnp.zeros((8, 128), F32)
        for k in range(8):
            inv = 1.0 / at[k, k]
            scale = jnp.where(sub == k, at[k, k], scale)
            m = [c * inv for c in col[k]]
            m[0] = jnp.where(sub > k, m[0], 0.0)
            for k2 in range(k + 1, 8):
                f = at[k, k2] * inv
                for k1 in range(k + 1, k2 + 1):
                    at[k1, k2] = at[k1, k2] - at[k, k1] * f
                for i in range(8 - n):
                    col[k2][i] = col[k2][i] - m[i] * at[k, k2]
            gp = jnp.broadcast_to(g[n][k:k + 1, :], (8, K))
            wp = jnp.broadcast_to(w[n][k:k + 1, :], (8, ROWS))
            for i in range(n, 8):
                g[i] = g[i] - m[i - n][:, :K] * gp
                w[i] = w[i] - jnp.concatenate([m[i - n], m[i - n]], axis=1) * wp
        root = lax.rsqrt(scale)
        r_ref[8 * n:8 * n + 8, :] = jnp.where(lane >= row + 8 * n, g[n] * root[:, :K], 0.0)
        basis_ref[8 * n:8 * n + 8, :] = w[n] * jnp.concatenate([root, root], axis=1)


def factor(gram, image):
    return pl.pallas_call(
        factor_kernel,
        out_shape=(jax.ShapeDtypeStruct((K, ROWS), F32), jax.ShapeDtypeStruct((K, K), F32)),
        name="cholesky_solve",
    )(gram, image)


def on_device(activations, start_basis):
    image, gram = comm(activations, start_basis.T)
    basis, rfactor = factor(gram.reshape(K, K), image)
    return (basis.T, rfactor)


def solution(mesh):
    in_specs = (P(("rows", "grp"), None), P(("rows", "grp"), None))
    out_specs = (P(("rows", "grp"), None), P())
    return jax.shard_map(
        on_device, mesh=mesh, in_specs=in_specs, out_specs=out_specs, check_vma=False
    )
```

```python
import functools
import math

import jax
import jax.numpy as jnp
from jax import lax
from jax.experimental import pallas as pl
from jax.experimental.pallas import tpu as pltpu
from jax.sharding import PartitionSpec as P

MESH = pl.DeviceIdType.MESH
F32 = jnp.float32
BF16 = jnp.bfloat16
ROWS, D, K = 256, 8192, 64
TOTAL = 131072
OWNERS = ((3, 13, 8, 9, 5, 7, 11, 10), (14, 6, 8, 9, 4, 12, 11, 10))
CHUNK = 512


def comm_kernel(a_hbm, s_hbm, img_ref, gram_ref, a_v, s_v, other, land_c, r1, land_1, r2, land_2, r3, land_z, pall,
                g_own, land_g, g_z, g_all,
                load_sem, c_send, c_recv, s1_send, s1_recv, s2_send, s2_recv, z_send, z_recv,
                zg_send, zg_recv, xy_send, xy_recv, f_send, f_recv,
                g1_send, g1_recv, g2_send, g2_recv, g3_send, g3_recv, know):
    r = lax.axis_index("rows")
    g = lax.axis_index("grp")
    x, z = r // 16, r % 16
    y, c = g // 2, g % 2

    def dev(xx, yy, zz, cc):
        return (xx * 16 + zz, yy * 2 + cc)

    partner = dev(x, y, z, 1 - c)

    def plane(k):
        return (x + k // 8) % 4, (y + (k // 2) % 4) % 4, (c + k % 2) % 2

    def remote(src, dst, ss, rs, target):
        return pltpu.make_async_remote_copy(src_ref=src, dst_ref=dst, send_sem=ss, recv_sem=rs, device_id=target,
                                            device_id_type=MESH)

    def arrived(ref, sem):
        pltpu.make_async_copy(ref, ref, sem).wait()

    me_a = (x, y)
    me_b = (y, x)
    steps = (2, 1, 3, 0)

    def chunk(half, q, t):
        return (c if half == 0 else 1 - c) * 8 + q * 4 + (me_a[q] + steps[t]) % 4

    def load(half, q, t):
        ch = chunk(half, q, t)
        src = a_hbm.at[:, pl.ds(pl.multiple_of(ch * CHUNK, CHUNK), CHUNK)]
        return pltpu.make_async_copy(src, a_v.at[ch], load_sem.at[t])

    bar = pltpu.get_barrier_semaphore()
    x_peers = [dev((x + k) % 4, y, z, c) for k in (1, 2, 3)]
    y_peers = [dev(x, (y + k) % 4, z, c) for k in (1, 2, 3)]

    def z_peers(k):
        return [dev(x, y, (z + k) % 16, c), dev(x, y, (z + 16 - k) % 16, c)]

    def greet(sem, targets):
        for target in targets:
            pl.semaphore_signal(sem, inc=1, device_id=target, device_id_type=MESH)

    greet(bar, [partner] + x_peers + y_peers + z_peers(1))

    load_s = pltpu.make_async_copy(s_hbm, s_v, load_sem.at[4])
    load_s.start()
    for t in range(4):
        for half in (1, 0):
            for q in range(2):
                load(half, q, t).start()

    load_s.wait()
    st = s_v[...]

    def partial(half, q, t, dst):
        part = jnp.dot(st, a_v[chunk(half, q, t)], preferred_element_type=F32)
        for s in range(4):
            for b in range(4):
                dst[q * 4 + s, (me_a[q] + steps[t]) % 4, b] = part[16 * s:16 * s + 16, 128 * b:128 * b + 128]

    def first_peer(q, k):
        return dev((x + k) % 4, y, z, c) if q == 0 else dev(x, (y + k) % 4, z, c)

    def second_peer(q, k):
        return first_peer(1 - q, k)

    def c_copy(q, t):
        a = (me_a[q] + steps[t]) % 4
        four = pl.ds(q * 4, 4)
        return remote(other.at[four, a], land_c.at[four, a], c_send, c_recv.at[t], partner)

    def first_axis(t):
        k = steps[t]
        arrived(land_c.at[pl.ds(0, 2)], c_recv.at[t])
        for q in range(2):
            a = (me_a[q] + k) % 4
            for s in range(4):
                i = q * 4 + s
                r1[i, a] = r1[i, a] + land_c[i, a]
                if k:
                    remote(r1.at[i, a], land_1.at[i, k - 1], s1_send, s1_recv.at[s], first_peer(q, k)).start()

    for t in range(4):
        arrived(a_v.at[pl.ds(0, 4)], load_sem.at[t])
        for q in range(2):
            partial(1, q, t, other)
        for q in range(2):
            partial(0, q, t, r1)
        if t == 0:
            pl.semaphore_wait(bar, 9)
        for q in range(2):
            c_copy(q, t).start()
        if t == 0:
            greet(know.at[0], y_peers)
            greet(know.at[1], z_peers(1))
        if t >= 1:
            first_axis(t - 1)
    first_axis(3)
    pl.semaphore_wait(know.at[0], 3)
    greet(know.at[2], [partner])
    pl.semaphore_wait(know.at[1], 2)
    greet(know.at[3], z_peers(2))
    pl.semaphore_wait(know.at[3], 2)
    greet(know.at[4], z_peers(4))

    for s in range(4):
        arrived(land_1.at[pl.ds(0, 2)], s1_recv.at[s])
        for q in range(2):
            i = q * 4 + s
            r2[i] = (r1[i, me_a[q]] + land_1[i, 0]) + (land_1[i, 1] + land_1[i, 2])
            for k in (1, 2, 3):
                remote(r2.at[i, (me_b[q] + k) % 4], land_2.at[i, k - 1], s2_send, s2_recv.at[s], second_peer(q, k)).start()

    owners = [jnp.where(c == 0, OWNERS[0][i], OWNERS[1][i]) for i in range(8)]

    def z_copy(i, slot):
        zo = owners[i]
        return remote(r3.at[i], land_z.at[slot], z_send, z_recv, dev(x, y, zo, c))

    for s in range(4):
        arrived(land_2.at[pl.ds(0, 2)], s2_recv.at[s])
        for q in range(2):
            i = q * 4 + s
            r3[i] = (r2[i, me_b[q]] + land_2[i, 0]) + (land_2[i, 1] + land_2[i, 2])
            if i == 0:
                pl.semaphore_wait(know.at[4], 2)
            zo = owners[i]

            @pl.when(zo != z)
            def _(i=i, zo=zo):
                z_copy(i, (zo - z + 16) % 16).start()

    my_i = sum(jnp.where(owners[i] == z, i, 0) for i in range(8))
    my_s, my_q = my_i % 4, my_i // 4
    owner = sum(jnp.where(owners[i] == z, 1, 0) for i in range(8)) == 1

    def place(q):
        return (c * 2 + q) * 16 + jnp.where(q == 0, x * 4 + y, y * 4 + x)

    def zg_copy(k):
        here = pall.at[place(my_q), my_s]
        return remote(here, here, zg_send, zg_recv.at[my_i], dev(x, y, (z + k) % 16, c))

    @pl.when(owner)
    def _():
        total = r3[my_i]
        arrived(land_z.at[pl.ds(1, 15)], z_recv)
        for k in range(1, 16):
            total = total + land_z[k]
        pall[place(my_q), my_s] = (total * (1.0 / math.sqrt(TOTAL))).astype(BF16)

        for k in (8, 7, 9, 6, 10, 5, 11, 4, 12, 3, 13, 2, 14, 1, 15):
            zg_copy(k).start()

    def far(k):
        return min(k // 4, 4 - k // 4) + min(k % 4, 4 - k % 4)

    def xy_copy(k, q, s):
        here = pall.at[place(q), s]
        return remote(here, here, xy_send, xy_recv.at[far(k) - 1], dev((x + k // 4) % 4, (y + k % 4) % 4, z, c))

    for i in (6, 7, 3, 2, 1, 5, 4, 0):
        q, s = i // 4, i % 4

        @pl.when(z != owners[i])
        def _(s=s, q=q):
            arrived(pall.at[place(q), s], zg_recv.at[q * 4 + s])

        for k in range(1, 16):
            xy_copy(k, q, s).start()

    def forward(k, q):
        xx, yy = (x - k // 4 + 4) % 4, (y - k % 4 + 4) % 4
        p = (c * 2 + q) * 16 + (xx * 4 + yy if q == 0 else yy * 4 + xx)
        return remote(pall.at[p], pall.at[p], f_send, f_recv, partner)

    for q in range(2):
        forward(0, q).start()

    for hops in range(1, 5):
        ring = [k for k in range(1, 16) if far(k) == hops]
        arrived(pall.at[pl.ds(0, 2 * len(ring))], xy_recv.at[hops - 1])
        for k in ring:
            for q in range(2):
                forward(k, q).start()

    def image_part(half, acc):
        for j in range(8):
            ch = half * 8 + j
            pt = jnp.concatenate([pall[ch * 4 + b].reshape(64, 128) for b in range(4)], axis=1)
            acc = acc + lax.dot_general(pt, a_v[ch], (((1,), (1,)), ((), ())), preferred_element_type=F32)
        return acc

    acc = image_part(c, jnp.zeros((K, ROWS), F32))
    theirs = pall.at[pl.ds((1 - c) * 32, 32)]
    arrived(theirs, f_recv)
    acc = image_part(1 - c, acc)
    img = acc * (1.0 / math.sqrt(D))
    img_ref[...] = img
    gram = lax.dot_general(img, img, (((1,), (1,)), ((), ())), precision=lax.Precision.HIGHEST, preferred_element_type=F32)
    gram = gram * (1.0 / TOTAL)

    for m in range(32):
        g_own[m] = gram[2 * m:2 * m + 2, :]
    me = (x * 4 + y) * 2 + c

    def g1_copy(k):
        xx, yy, cc = plane(k)
        return remote(g_own.at[(xx * 4 + yy) * 2 + cc], land_g.at[k], g1_send, g1_recv, dev(xx, yy, z, cc))

    pl.semaphore_wait(know.at[2], 1)
    for k in range(1, 32):
        g1_copy(k).start()

    arrived(other, c_send)
    arrived(r1.at[pl.ds(0, 6)], s1_send)
    arrived(r2.at[pl.ds(0, 6)], s2_send)

    @pl.when(owner)
    def _():
        arrived(r3.at[pl.ds(0, 7)], z_send)
        arrived(land_z.at[pl.ds(0, 15), pl.ds(0, 8)], zg_send)

    @pl.when(jnp.logical_not(owner))
    def _():
        arrived(r3, z_send)

    arrived(pall.at[pl.ds(0, 30)], xy_send)
    arrived(theirs, f_send)

    most = land_g.at[pl.ds(1, 31)]
    arrived(most, g1_recv)
    g_z[z] = g_own[me] + jnp.sum(land_g[1:32], axis=0)

    def g2_copy(k):
        return remote(g_z.at[z], g_z.at[z], g2_send, g2_recv, dev(x, y, (z + k) % 16, c))

    for k in (8, 7, 9, 6, 10, 5, 11, 4, 12, 3, 13, 2, 14, 1, 15):
        g2_copy(k).start()
    arrived(most, g1_send)
    line = g_z.at[pl.ds(0, 15)]
    arrived(line, g2_recv)
    g_all[me] = jnp.sum(g_z[...], axis=0)

    def g3_copy(k):
        xx, yy, cc = plane(k)
        return remote(g_all.at[me], g_all.at[me], g3_send, g3_recv, dev(xx, yy, z, cc))

    for k in range(1, 32):
        g3_copy(k).start()
    arrived(line, g2_send)
    others = g_all.at[pl.ds(0, 31)]
    arrived(others, g3_recv)
    gram_ref[...] = g_all[...]
    arrived(others, g3_send)


def comm(activations, start_basis):
    dma = pltpu.SemaphoreType.DMA
    return pl.pallas_call(
        comm_kernel,
        out_shape=(jax.ShapeDtypeStruct((K, ROWS), F32), jax.ShapeDtypeStruct((32, 2, K), F32)),
        in_specs=[pl.BlockSpec(memory_space=pl.ANY)] * 2,
        out_specs=(pl.BlockSpec(memory_space=pltpu.VMEM),) * 2,
        scratch_shapes=[
            pltpu.VMEM((16, ROWS, CHUNK), BF16),
            pltpu.VMEM((K, ROWS), BF16),
            pltpu.VMEM((8, 4, 4, 16, 128), F32),
            pltpu.VMEM((8, 4, 4, 16, 128), F32),
            pltpu.VMEM((8, 4, 4, 16, 128), F32),
            pltpu.VMEM((8, 3, 4, 16, 128), F32),
            pltpu.VMEM((8, 4, 16, 128), F32),
            pltpu.VMEM((8, 3, 16, 128), F32),
            pltpu.VMEM((8, 16, 128), F32),
            pltpu.VMEM((16, 16, 128), F32),
            pltpu.VMEM((64, 4, 16, 128), BF16),
            pltpu.VMEM((32, 2, K), F32),
            pltpu.VMEM((32, 2, K), F32),
            pltpu.VMEM((16, 2, K), F32),
            pltpu.VMEM((32, 2, K), F32),
            dma((5,)), dma, dma((4,)), dma, dma((4,)), dma, dma((4,)), dma, dma,
            dma, dma((8,)), dma, dma((4,)), dma, dma,
            dma, dma, dma, dma, dma, dma, pltpu.SemaphoreType.REGULAR((5,)),
        ],
        compiler_params=pltpu.CompilerParams(collective_id=0, has_side_effects=True, vmem_limit_bytes=60 << 20),
        cost_estimate=pl.CostEstimate(flops=4 * ROWS * D * K, bytes_accessed=ROWS * D * 2, transcendentals=0),
        name="reduce_project_gram",
    )(activations, start_basis)


def factor_kernel(gram_ref, img_ref, basis_ref, r_ref):
    g = [gram_ref[8 * i:8 * i + 8, :] for i in range(8)]
    w = [img_ref[8 * i:8 * i + 8, :] for i in range(8)]
    sub = lax.broadcasted_iota(jnp.int32, (8, 128), 0)
    lane = lax.broadcasted_iota(jnp.int32, (8, K), 1)
    row = lax.broadcasted_iota(jnp.int32, (8, K), 0)
    for n in range(8):
        col = [[jnp.broadcast_to(g[i][:, 8 * n + k:8 * n + k + 1], (8, 128)) for i in range(n, 8)] for k in range(8)]
        at = {(h, k): jnp.broadcast_to(col[k][0][h:h + 1, :], (8, 128)) for k in range(8) for h in range(k + 1)}
        scale = jnp.zeros((8, 128), F32)
        for k in range(8):
            inv = 1.0 / at[k, k]
            scale = jnp.where(sub == k, at[k, k], scale)
            m = [c * inv for c in col[k]]
            m[0] = jnp.where(sub > k, m[0], 0.0)
            for k2 in range(k + 1, 8):
                f = at[k, k2] * inv
                for k1 in range(k + 1, k2 + 1):
                    at[k1, k2] = at[k1, k2] - at[k, k1] * f
                for i in range(8 - n):
                    col[k2][i] = col[k2][i] - m[i] * at[k, k2]
            gp = jnp.broadcast_to(g[n][k:k + 1, :], (8, K))
            wp = jnp.broadcast_to(w[n][k:k + 1, :], (8, ROWS))
            for i in range(n, 8):
                g[i] = g[i] - m[i - n][:, :K] * gp
                w[i] = w[i] - jnp.concatenate([m[i - n], m[i - n]], axis=1) * wp
        root = lax.rsqrt(scale)
        r_ref[8 * n:8 * n + 8, :] = jnp.where(lane >= row + 8 * n, g[n] * root[:, :K], 0.0)
        basis_ref[8 * n:8 * n + 8, :] = w[n] * jnp.concatenate([root, root], axis=1)


def factor(gram, image):
    return pl.pallas_call(
        factor_kernel,
        out_shape=(jax.ShapeDtypeStruct((K, ROWS), F32), jax.ShapeDtypeStruct((K, K), F32)),
        name="cholesky_solve",
    )(gram, image)


def on_device(activations, start_basis):
    image, gram = comm(activations, start_basis.T)
    basis, rfactor = factor(gram.reshape(K, K), image)
    return (basis.T, rfactor)


def solution(mesh):
    in_specs = (P(("rows", "grp"), None), P(("rows", "grp"), None))
    out_specs = (P(("rows", "grp"), None), P())
    return jax.shard_map(
        on_device, mesh=mesh, in_specs=in_specs, out_specs=out_specs, check_vma=False
    )
```

```python
import functools
import math

import jax
import jax.numpy as jnp
from jax import lax
from jax.experimental import pallas as pl
from jax.experimental.pallas import tpu as pltpu
from jax.sharding import PartitionSpec as P

MESH = pl.DeviceIdType.MESH
F32 = jnp.float32
BF16 = jnp.bfloat16
ROWS, D, K = 256, 8192, 64
TOTAL = 131072
OWNERS = ((3, 13, 8, 9, 5, 7, 11, 10), (14, 6, 8, 9, 4, 12, 11, 10))
CHUNK = 512


def comm_kernel(a_hbm, s_hbm, img_ref, gram_ref, a_v, s_v, other, land_c, r1, out_1, land_1, r2, land_2, r3, land_z, pall,
                g_own, land_g, g_z, g_all,
                load_sem, c_send, c_recv, s1_send, s1_recv, s2_send, s2_recv, z_send, z_recv,
                zg_send, zg_recv, xy_send, xy_recv, f_send, f_recv,
                g1_send, g1_recv, g2_send, g2_recv, g3_send, g3_recv, know):
    r = lax.axis_index("rows")
    g = lax.axis_index("grp")
    x, z = r // 16, r % 16
    y, c = g // 2, g % 2

    def dev(xx, yy, zz, cc):
        return (xx * 16 + zz, yy * 2 + cc)

    partner = dev(x, y, z, 1 - c)

    def plane(k):
        return (x + k // 8) % 4, (y + (k // 2) % 4) % 4, (c + k % 2) % 2

    def remote(src, dst, ss, rs, target):
        return pltpu.make_async_remote_copy(src_ref=src, dst_ref=dst, send_sem=ss, recv_sem=rs, device_id=target,
                                            device_id_type=MESH)

    def arrived(ref, sem):
        pltpu.make_async_copy(ref, ref, sem).wait()

    me_a = (x, y)
    me_b = (y, x)
    steps = (2, 1, 3, 0)

    def chunk(half, q, t):
        return (c if half == 0 else 1 - c) * 8 + q * 4 + (me_a[q] + steps[t]) % 4

    def load(half, q, t):
        ch = chunk(half, q, t)
        src = a_hbm.at[:, pl.ds(pl.multiple_of(ch * CHUNK, CHUNK), CHUNK)]
        return pltpu.make_async_copy(src, a_v.at[ch], load_sem.at[t])

    bar = pltpu.get_barrier_semaphore()
    x_peers = [dev((x + k) % 4, y, z, c) for k in (1, 2, 3)]
    y_peers = [dev(x, (y + k) % 4, z, c) for k in (1, 2, 3)]

    def z_peers(k):
        return [dev(x, y, (z + k) % 16, c), dev(x, y, (z + 16 - k) % 16, c)]

    def greet(sem, targets):
        for target in targets:
            pl.semaphore_signal(sem, inc=1, device_id=target, device_id_type=MESH)

    greet(bar, [partner] + x_peers + y_peers + z_peers(1))

    load_s = pltpu.make_async_copy(s_hbm, s_v, load_sem.at[4])
    load_s.start()
    for t in range(4):
        for half in (1, 0):
            for q in range(2):
                load(half, q, t).start()

    load_s.wait()
    st = s_v[...]

    def partial(half, q, t, dst):
        part = jnp.dot(st, a_v[chunk(half, q, t)], preferred_element_type=F32)
        for s in range(4):
            for b in range(4):
                dst[q * 4 + s, (me_a[q] + steps[t]) % 4, b] = part[16 * s:16 * s + 16, 128 * b:128 * b + 128]

    def first_peer(q, k):
        return dev((x + k) % 4, y, z, c) if q == 0 else dev(x, (y + k) % 4, z, c)

    def second_peer(q, k):
        return first_peer(1 - q, k)

    def c_copy(q, t):
        a = (me_a[q] + steps[t]) % 4
        four = pl.ds(q * 4, 4)
        return remote(other.at[four, a], land_c.at[four, a], c_send, c_recv.at[t], partner)

    def first_axis(t):
        k = steps[t]
        arrived(land_c.at[pl.ds(0, 2)], c_recv.at[t])
        for q in range(2):
            a = (me_a[q] + k) % 4
            for s in range(4):
                i = q * 4 + s
                part = r1[i, a] + land_c[i, a]
                if k == 0:
                    r1[i, a] = part
                else:
                    out_1[i, a] = part.astype(BF16)
                    remote(out_1.at[i, a], land_1.at[i, k - 1], s1_send, s1_recv.at[s], first_peer(q, k)).start()

    for t in range(4):
        arrived(a_v.at[pl.ds(0, 4)], load_sem.at[t])
        for q in range(2):
            partial(1, q, t, other)
        for q in range(2):
            partial(0, q, t, r1)
        if t == 0:
            pl.semaphore_wait(bar, 9)
        for q in range(2):
            c_copy(q, t).start()
        if t == 0:
            greet(know.at[0], y_peers)
            greet(know.at[1], z_peers(1))
        if t >= 1:
            first_axis(t - 1)
    first_axis(3)
    pl.semaphore_wait(know.at[0], 3)
    greet(know.at[2], [partner])
    pl.semaphore_wait(know.at[1], 2)
    greet(know.at[3], z_peers(2))
    pl.semaphore_wait(know.at[3], 2)
    greet(know.at[4], z_peers(4))

    for s in range(4):
        arrived(land_1.at[pl.ds(0, 2)], s1_recv.at[s])
        for q in range(2):
            i = q * 4 + s
            r2[i] = (r1[i, me_a[q]] + land_1[i, 0].astype(F32)) + (land_1[i, 1].astype(F32) + land_1[i, 2].astype(F32))
            for k in (1, 2, 3):
                remote(r2.at[i, (me_b[q] + k) % 4], land_2.at[i, k - 1], s2_send, s2_recv.at[s], second_peer(q, k)).start()

    owners = [jnp.where(c == 0, OWNERS[0][i], OWNERS[1][i]) for i in range(8)]

    def z_copy(i, slot):
        zo = owners[i]
        return remote(r3.at[i], land_z.at[slot], z_send, z_recv, dev(x, y, zo, c))

    for s in range(4):
        arrived(land_2.at[pl.ds(0, 2)], s2_recv.at[s])
        for q in range(2):
            i = q * 4 + s
            r3[i] = (r2[i, me_b[q]] + land_2[i, 0]) + (land_2[i, 1] + land_2[i, 2])
            if i == 0:
                pl.semaphore_wait(know.at[4], 2)
            zo = owners[i]

            @pl.when(zo != z)
            def _(i=i, zo=zo):
                z_copy(i, (zo - z + 16) % 16).start()

    my_i = sum(jnp.where(owners[i] == z, i, 0) for i in range(8))
    my_s, my_q = my_i % 4, my_i // 4
    owner = sum(jnp.where(owners[i] == z, 1, 0) for i in range(8)) == 1

    def place(q):
        return (c * 2 + q) * 16 + jnp.where(q == 0, x * 4 + y, y * 4 + x)

    def zg_copy(k):
        here = pall.at[place(my_q), my_s]
        return remote(here, here, zg_send, zg_recv.at[my_i], dev(x, y, (z + k) % 16, c))

    @pl.when(owner)
    def _():
        total = r3[my_i]
        arrived(land_z.at[pl.ds(1, 15)], z_recv)
        for k in range(1, 16):
            total = total + land_z[k]
        pall[place(my_q), my_s] = (total * (1.0 / math.sqrt(TOTAL))).astype(BF16)

        for k in (8, 7, 9, 6, 10, 5, 11, 4, 12, 3, 13, 2, 14, 1, 15):
            zg_copy(k).start()

    def far(k):
        return min(k // 4, 4 - k // 4) + min(k % 4, 4 - k % 4)

    def xy_copy(k, q, s):
        here = pall.at[place(q), s]
        return remote(here, here, xy_send, xy_recv.at[far(k) - 1], dev((x + k // 4) % 4, (y + k % 4) % 4, z, c))

    for i in (6, 7, 3, 2, 1, 5, 4, 0):
        q, s = i // 4, i % 4

        @pl.when(z != owners[i])
        def _(s=s, q=q):
            arrived(pall.at[place(q), s], zg_recv.at[q * 4 + s])

        for k in range(1, 16):
            xy_copy(k, q, s).start()

    def forward(k, q):
        xx, yy = (x - k // 4 + 4) % 4, (y - k % 4 + 4) % 4
        p = (c * 2 + q) * 16 + (xx * 4 + yy if q == 0 else yy * 4 + xx)
        return remote(pall.at[p], pall.at[p], f_send, f_recv, partner)

    for q in range(2):
        forward(0, q).start()

    for hops in range(1, 5):
        ring = [k for k in range(1, 16) if far(k) == hops]
        arrived(pall.at[pl.ds(0, 2 * len(ring))], xy_recv.at[hops - 1])
        for k in ring:
            for q in range(2):
                forward(k, q).start()

    def image_part(half, acc):
        for j in range(8):
            ch = half * 8 + j
            pt = jnp.concatenate([pall[ch * 4 + b].reshape(64, 128) for b in range(4)], axis=1)
            acc = acc + lax.dot_general(pt, a_v[ch], (((1,), (1,)), ((), ())), preferred_element_type=F32)
        return acc

    acc = image_part(c, jnp.zeros((K, ROWS), F32))
    theirs = pall.at[pl.ds((1 - c) * 32, 32)]
    arrived(theirs, f_recv)
    acc = image_part(1 - c, acc)
    img = acc * (1.0 / math.sqrt(D))
    img_ref[...] = img
    gram = lax.dot_general(img, img, (((1,), (1,)), ((), ())), precision=lax.Precision.HIGHEST, preferred_element_type=F32)
    gram = gram * (1.0 / TOTAL)

    for m in range(32):
        g_own[m] = gram[2 * m:2 * m + 2, :]
    me = (x * 4 + y) * 2 + c

    def g1_copy(k):
        xx, yy, cc = plane(k)
        return remote(g_own.at[(xx * 4 + yy) * 2 + cc], land_g.at[k], g1_send, g1_recv, dev(xx, yy, z, cc))

    pl.semaphore_wait(know.at[2], 1)
    for k in range(1, 32):
        g1_copy(k).start()

    arrived(other, c_send)
    arrived(out_1.at[pl.ds(0, 6)], s1_send)
    arrived(r2.at[pl.ds(0, 6)], s2_send)

    @pl.when(owner)
    def _():
        arrived(r3.at[pl.ds(0, 7)], z_send)
        arrived(land_z.at[pl.ds(0, 15), pl.ds(0, 8)], zg_send)

    @pl.when(jnp.logical_not(owner))
    def _():
        arrived(r3, z_send)

    arrived(pall.at[pl.ds(0, 30)], xy_send)
    arrived(theirs, f_send)

    most = land_g.at[pl.ds(1, 31)]
    arrived(most, g1_recv)
    g_z[z] = g_own[me] + jnp.sum(land_g[1:32], axis=0)

    def g2_copy(k):
        return remote(g_z.at[z], g_z.at[z], g2_send, g2_recv, dev(x, y, (z + k) % 16, c))

    for k in (8, 7, 9, 6, 10, 5, 11, 4, 12, 3, 13, 2, 14, 1, 15):
        g2_copy(k).start()
    arrived(most, g1_send)
    line = g_z.at[pl.ds(0, 15)]
    arrived(line, g2_recv)
    g_all[me] = jnp.sum(g_z[...], axis=0)

    def g3_copy(k):
        xx, yy, cc = plane(k)
        return remote(g_all.at[me], g_all.at[me], g3_send, g3_recv, dev(xx, yy, z, cc))

    for k in range(1, 32):
        g3_copy(k).start()
    arrived(line, g2_send)
    others = g_all.at[pl.ds(0, 31)]
    arrived(others, g3_recv)
    gram_ref[...] = g_all[...]
    arrived(others, g3_send)


def comm(activations, start_basis):
    dma = pltpu.SemaphoreType.DMA
    return pl.pallas_call(
        comm_kernel,
        out_shape=(jax.ShapeDtypeStruct((K, ROWS), F32), jax.ShapeDtypeStruct((32, 2, K), F32)),
        in_specs=[pl.BlockSpec(memory_space=pl.ANY)] * 2,
        out_specs=(pl.BlockSpec(memory_space=pltpu.VMEM),) * 2,
        scratch_shapes=[
            pltpu.VMEM((16, ROWS, CHUNK), BF16),
            pltpu.VMEM((K, ROWS), BF16),
            pltpu.VMEM((8, 4, 4, 16, 128), F32),
            pltpu.VMEM((8, 4, 4, 16, 128), F32),
            pltpu.VMEM((8, 4, 4, 16, 128), F32),
            pltpu.VMEM((8, 4, 4, 16, 128), BF16),
            pltpu.VMEM((8, 3, 4, 16, 128), BF16),
            pltpu.VMEM((8, 4, 16, 128), F32),
            pltpu.VMEM((8, 3, 16, 128), F32),
            pltpu.VMEM((8, 16, 128), F32),
            pltpu.VMEM((16, 16, 128), F32),
            pltpu.VMEM((64, 4, 16, 128), BF16),
            pltpu.VMEM((32, 2, K), F32),
            pltpu.VMEM((32, 2, K), F32),
            pltpu.VMEM((16, 2, K), F32),
            pltpu.VMEM((32, 2, K), F32),
            dma((5,)), dma, dma((4,)), dma, dma((4,)), dma, dma((4,)), dma, dma,
            dma, dma((8,)), dma, dma((4,)), dma, dma,
            dma, dma, dma, dma, dma, dma, pltpu.SemaphoreType.REGULAR((5,)),
        ],
        compiler_params=pltpu.CompilerParams(collective_id=0, has_side_effects=True, vmem_limit_bytes=60 << 20),
        cost_estimate=pl.CostEstimate(flops=4 * ROWS * D * K, bytes_accessed=ROWS * D * 2, transcendentals=0),
        name="reduce_project_gram",
    )(activations, start_basis)


def factor_kernel(gram_ref, img_ref, basis_ref, r_ref):
    g = [gram_ref[8 * i:8 * i + 8, :] for i in range(8)]
    w = [img_ref[8 * i:8 * i + 8, :] for i in range(8)]
    sub = lax.broadcasted_iota(jnp.int32, (8, 128), 0)
    lane = lax.broadcasted_iota(jnp.int32, (8, K), 1)
    row = lax.broadcasted_iota(jnp.int32, (8, K), 0)
    for n in range(8):
        col = [[jnp.broadcast_to(g[i][:, 8 * n + k:8 * n + k + 1], (8, 128)) for i in range(n, 8)] for k in range(8)]
        at = {(h, k): jnp.broadcast_to(col[k][0][h:h + 1, :], (8, 128)) for k in range(8) for h in range(k + 1)}
        scale = jnp.zeros((8, 128), F32)
        for k in range(8):
            inv = 1.0 / at[k, k]
            scale = jnp.where(sub == k, at[k, k], scale)
            m = [c * inv for c in col[k]]
            m[0] = jnp.where(sub > k, m[0], 0.0)
            for k2 in range(k + 1, 8):
                f = at[k, k2] * inv
                for k1 in range(k + 1, k2 + 1):
                    at[k1, k2] = at[k1, k2] - at[k, k1] * f
                for i in range(8 - n):
                    col[k2][i] = col[k2][i] - m[i] * at[k, k2]
            gp = jnp.broadcast_to(g[n][k:k + 1, :], (8, K))
            wp = jnp.broadcast_to(w[n][k:k + 1, :], (8, ROWS))
            for i in range(n, 8):
                g[i] = g[i] - m[i - n][:, :K] * gp
                w[i] = w[i] - jnp.concatenate([m[i - n], m[i - n]], axis=1) * wp
        root = lax.rsqrt(scale)
        r_ref[8 * n:8 * n + 8, :] = jnp.where(lane >= row + 8 * n, g[n] * root[:, :K], 0.0)
        basis_ref[8 * n:8 * n + 8, :] = w[n] * jnp.concatenate([root, root], axis=1)


def factor(gram, image):
    return pl.pallas_call(
        factor_kernel,
        out_shape=(jax.ShapeDtypeStruct((K, ROWS), F32), jax.ShapeDtypeStruct((K, K), F32)),
        name="cholesky_solve",
    )(gram, image)


def on_device(activations, start_basis):
    image, gram = comm(activations, start_basis.T)
    basis, rfactor = factor(gram.reshape(K, K), image)
    return (basis.T, rfactor)


def solution(mesh):
    in_specs = (P(("rows", "grp"), None), P(("rows", "grp"), None))
    out_specs = (P(("rows", "grp"), None), P())
    return jax.shard_map(
        on_device, mesh=mesh, in_specs=in_specs, out_specs=out_specs, check_vma=False
    )
```

```python
import functools
import math

import jax
import jax.numpy as jnp
from jax import lax
from jax.experimental import pallas as pl
from jax.experimental.pallas import tpu as pltpu
from jax.sharding import PartitionSpec as P

MESH = pl.DeviceIdType.MESH
F32 = jnp.float32
BF16 = jnp.bfloat16
ROWS, D, K = 256, 8192, 64
TOTAL = 131072
OWNERS = ((3, 13, 8, 9, 5, 7, 11, 10), (14, 6, 8, 9, 4, 12, 11, 10))
CHUNK = 512


def comm_kernel(a_hbm, s_hbm, img_ref, gram_ref, a_v, s_v, other, land_c, r1, out_1, land_1, r2, land_2, r3, land_z, pall,
                g_own, land_g, g_z, g_all,
                load_sem, c_send, c_recv, s1_send, s1_recv, s2_send, s2_recv, z_send, z_recv,
                zg_send, zg_recv, xy_send, xy_recv, f_send, f_recv,
                g1_send, g1_recv, g2_send, g2_recv, g3_send, g3_recv, know):
    r = lax.axis_index("rows")
    g = lax.axis_index("grp")
    x, z = r // 16, r % 16
    y, c = g // 2, g % 2

    def dev(xx, yy, zz, cc):
        return (xx * 16 + zz, yy * 2 + cc)

    partner = dev(x, y, z, 1 - c)

    def plane(k):
        return (x + k // 8) % 4, (y + (k // 2) % 4) % 4, (c + k % 2) % 2

    def remote(src, dst, ss, rs, target):
        return pltpu.make_async_remote_copy(src_ref=src, dst_ref=dst, send_sem=ss, recv_sem=rs, device_id=target,
                                            device_id_type=MESH)

    def arrived(ref, sem):
        pltpu.make_async_copy(ref, ref, sem).wait()

    me_a = (x, y)
    me_b = (y, x)
    steps = (2, 1, 3, 0)

    def chunk(half, q, t):
        return (c if half == 0 else 1 - c) * 8 + q * 4 + (me_a[q] + steps[t]) % 4

    def load(half, q, t):
        ch = chunk(half, q, t)
        src = a_hbm.at[:, pl.ds(pl.multiple_of(ch * CHUNK, CHUNK), CHUNK)]
        return pltpu.make_async_copy(src, a_v.at[ch], load_sem.at[t])

    bar = pltpu.get_barrier_semaphore()
    x_peers = [dev((x + k) % 4, y, z, c) for k in (1, 2, 3)]
    y_peers = [dev(x, (y + k) % 4, z, c) for k in (1, 2, 3)]

    def z_peers(k):
        return [dev(x, y, (z + k) % 16, c), dev(x, y, (z + 16 - k) % 16, c)]

    def greet(sem, targets):
        for target in targets:
            pl.semaphore_signal(sem, inc=1, device_id=target, device_id_type=MESH)

    greet(bar, [partner] + x_peers + y_peers + z_peers(1))

    load_s = pltpu.make_async_copy(s_hbm, s_v, load_sem.at[4])
    load_s.start()
    for t in range(4):
        for half in (1, 0):
            for q in range(2):
                load(half, q, t).start()

    load_s.wait()
    st = s_v[...]

    def partial(half, q, t, dst):
        part = jnp.dot(st, a_v[chunk(half, q, t)], preferred_element_type=F32)
        for s in range(4):
            for b in range(4):
                dst[q * 4 + s, (me_a[q] + steps[t]) % 4, b] = part[16 * s:16 * s + 16, 128 * b:128 * b + 128]

    def first_peer(q, k):
        return dev((x + k) % 4, y, z, c) if q == 0 else dev(x, (y + k) % 4, z, c)

    def second_peer(q, k):
        return first_peer(1 - q, k)

    def c_copy(q, t):
        a = (me_a[q] + steps[t]) % 4
        four = pl.ds(q * 4, 4)
        return remote(other.at[four, a], land_c.at[four, a], c_send, c_recv.at[t], partner)

    def first_axis(t):
        k = steps[t]
        arrived(land_c.at[pl.ds(0, 2)], c_recv.at[t])
        for q in range(2):
            a = (me_a[q] + k) % 4
            for s in range(4):
                i = q * 4 + s
                part = r1[i, a] + land_c[i, a]
                if k == 0:
                    r1[i, a] = part
                else:
                    out_1[i, a] = part.astype(BF16)
                    remote(out_1.at[i, a], land_1.at[i, k - 1], s1_send, s1_recv.at[s], first_peer(q, k)).start()

    for t in range(4):
        arrived(a_v.at[pl.ds(0, 4)], load_sem.at[t])
        for q in range(2):
            partial(1, q, t, other)
        for q in range(2):
            partial(0, q, t, r1)
        if t == 0:
            pl.semaphore_wait(bar, 9)
        for q in range(2):
            c_copy(q, t).start()
        if t == 0:
            greet(know.at[0], y_peers)
            greet(know.at[1], z_peers(1))
        if t >= 1:
            first_axis(t - 1)
    first_axis(3)
    pl.semaphore_wait(know.at[0], 3)
    greet(know.at[2], [partner])
    pl.semaphore_wait(know.at[1], 2)
    greet(know.at[3], z_peers(2))
    pl.semaphore_wait(know.at[3], 2)
    greet(know.at[4], z_peers(4))

    for s in range(4):
        arrived(land_1.at[pl.ds(0, 2)], s1_recv.at[s])
        for q in range(2):
            i = q * 4 + s
            r2[i] = (r1[i, me_a[q]] + land_1[i, 0].astype(F32)) + (land_1[i, 1].astype(F32) + land_1[i, 2].astype(F32))
            for k in (1, 2, 3):
                remote(r2.at[i, (me_b[q] + k) % 4], land_2.at[i, k - 1], s2_send, s2_recv.at[s], second_peer(q, k)).start()

    owners = [jnp.where(c == 0, OWNERS[0][i], OWNERS[1][i]) for i in range(8)]

    def z_copy(i, slot):
        zo = owners[i]
        return remote(r3.at[i], land_z.at[slot], z_send, z_recv, dev(x, y, zo, c))

    for s in range(4):
        arrived(land_2.at[pl.ds(0, 2)], s2_recv.at[s])
        for q in range(2):
            i = q * 4 + s
            r3[i] = (r2[i, me_b[q]] + land_2[i, 0]) + (land_2[i, 1] + land_2[i, 2])
            if i == 0:
                pl.semaphore_wait(know.at[4], 2)
            zo = owners[i]

            @pl.when(zo != z)
            def _(i=i, zo=zo):
                z_copy(i, (zo - z + 16) % 16).start()

    my_i = sum(jnp.where(owners[i] == z, i, 0) for i in range(8))
    my_s, my_q = my_i % 4, my_i // 4
    owner = sum(jnp.where(owners[i] == z, 1, 0) for i in range(8)) == 1

    def place(q):
        return (c * 2 + q) * 16 + jnp.where(q == 0, x * 4 + y, y * 4 + x)

    def zg_copy(k):
        here = pall.at[place(my_q), my_s]
        return remote(here, here, zg_send, zg_recv.at[my_i], dev(x, y, (z + k) % 16, c))

    @pl.when(owner)
    def _():
        total = r3[my_i]
        arrived(land_z.at[pl.ds(1, 15)], z_recv)
        for k in range(1, 16):
            total = total + land_z[k]
        pall[place(my_q), my_s] = (total * (1.0 / math.sqrt(TOTAL))).astype(BF16)

        for k in (8, 7, 9, 6, 10, 5, 11, 4, 12, 3, 13, 2, 14, 1, 15):
            zg_copy(k).start()

    def far(k):
        return min(k // 4, 4 - k // 4) + min(k % 4, 4 - k % 4)

    def xy_copy(k, q, s):
        here = pall.at[place(q), s]
        return remote(here, here, xy_send, xy_recv.at[far(k) - 1], dev((x + k // 4) % 4, (y + k % 4) % 4, z, c))

    for i in (6, 7, 3, 2, 1, 5, 4, 0):
        q, s = i // 4, i % 4

        @pl.when(z != owners[i])
        def _(s=s, q=q):
            arrived(pall.at[place(q), s], zg_recv.at[q * 4 + s])

        for k in range(1, 16):
            xy_copy(k, q, s).start()

    def forward(k, q):
        xx, yy = (x - k // 4 + 4) % 4, (y - k % 4 + 4) % 4
        p = (c * 2 + q) * 16 + (xx * 4 + yy if q == 0 else yy * 4 + xx)
        return remote(pall.at[p], pall.at[p], f_send, f_recv, partner)

    for q in range(2):
        forward(0, q).start()

    for hops in range(1, 5):
        ring = [k for k in range(1, 16) if far(k) == hops]
        arrived(pall.at[pl.ds(0, 2 * len(ring))], xy_recv.at[hops - 1])
        for k in ring:
            for q in range(2):
                forward(k, q).start()

    def image_part(half, acc):
        for j in range(8):
            ch = half * 8 + j
            pt = jnp.concatenate([pall[ch * 4 + b].reshape(64, 128) for b in range(4)], axis=1)
            acc = acc + lax.dot_general(pt, a_v[ch], (((1,), (1,)), ((), ())), preferred_element_type=F32)
        return acc

    acc = image_part(c, jnp.zeros((K, ROWS), F32))
    theirs = pall.at[pl.ds((1 - c) * 32, 32)]
    arrived(theirs, f_recv)
    acc = image_part(1 - c, acc)
    img = acc * (1.0 / math.sqrt(D))
    img_ref[...] = img
    gram = lax.dot_general(img, img, (((1,), (1,)), ((), ())), precision=lax.Precision.HIGHEST, preferred_element_type=F32)
    gram = gram * (1.0 / TOTAL)

    for m in range(8):
        g_own[m] = jnp.concatenate([gram[8 * m:8 * m + 4, :], gram[8 * m + 4:8 * m + 8, :]], axis=1)
    me = y * 2 + c
    seat = x * 8 + me

    def g1_copy(k):
        xx, yy, cc = plane(k)
        return remote(g_own.at[yy * 2 + cc], land_g.at[seat], g1_send, g1_recv, dev(xx, yy, z, cc))

    pl.semaphore_wait(know.at[2], 1)
    for k in range(1, 32):
        g1_copy(k).start()

    arrived(other, c_send)
    arrived(out_1.at[pl.ds(0, 6)], s1_send)
    arrived(r2.at[pl.ds(0, 6)], s2_send)

    @pl.when(owner)
    def _():
        arrived(r3.at[pl.ds(0, 7)], z_send)
        arrived(land_z.at[pl.ds(0, 15), pl.ds(0, 8)], zg_send)

    @pl.when(jnp.logical_not(owner))
    def _():
        arrived(r3, z_send)

    arrived(pall.at[pl.ds(0, 30)], xy_send)
    arrived(theirs, f_send)

    land_g[seat] = g_own[me]
    most = land_g.at[pl.ds(0, 31)]
    arrived(most, g1_recv)
    g_z[z] = jnp.sum(land_g[...], axis=0)

    def g2_copy(k):
        return remote(g_z.at[z], g_z.at[z], g2_send, g2_recv, dev(x, y, (z + k) % 16, c))

    for k in (8, 7, 9, 6, 10, 5, 11, 4, 12, 3, 13, 2, 14, 1, 15):
        g2_copy(k).start()
    arrived(most, g1_send)
    line = g_z.at[pl.ds(0, 15)]
    arrived(line, g2_recv)
    g_all[me] = jnp.sum(g_z[...], axis=0)

    def g3_copy(k):
        xx, yy, cc = plane(k)
        return remote(g_all.at[me], g_all.at[me], g3_send, g3_recv, dev(xx, yy, z, cc))

    for k in range(1, 8):
        g3_copy(k).start()
    arrived(line, g2_send)
    others = g_all.at[pl.ds(0, 7)]
    arrived(others, g3_recv)
    gram_ref[...] = g_all[...]
    arrived(others, g3_send)


def comm(activations, start_basis):
    dma = pltpu.SemaphoreType.DMA
    return pl.pallas_call(
        comm_kernel,
        out_shape=(jax.ShapeDtypeStruct((K, ROWS), F32), jax.ShapeDtypeStruct((8, 4, 128), F32)),
        in_specs=[pl.BlockSpec(memory_space=pl.ANY)] * 2,
        out_specs=(pl.BlockSpec(memory_space=pltpu.VMEM),) * 2,
        scratch_shapes=[
            pltpu.VMEM((16, ROWS, CHUNK), BF16),
            pltpu.VMEM((K, ROWS), BF16),
            pltpu.VMEM((8, 4, 4, 16, 128), F32),
            pltpu.VMEM((8, 4, 4, 16, 128), F32),
            pltpu.VMEM((8, 4, 4, 16, 128), F32),
            pltpu.VMEM((8, 4, 4, 16, 128), BF16),
            pltpu.VMEM((8, 3, 4, 16, 128), BF16),
            pltpu.VMEM((8, 4, 16, 128), F32),
            pltpu.VMEM((8, 3, 16, 128), F32),
            pltpu.VMEM((8, 16, 128), F32),
            pltpu.VMEM((16, 16, 128), F32),
            pltpu.VMEM((64, 4, 16, 128), BF16),
            pltpu.VMEM((8, 4, 128), F32),
            pltpu.VMEM((32, 4, 128), F32),
            pltpu.VMEM((16, 4, 128), F32),
            pltpu.VMEM((8, 4, 128), F32),
            dma((5,)), dma, dma((4,)), dma, dma((4,)), dma, dma((4,)), dma, dma,
            dma, dma((8,)), dma, dma((4,)), dma, dma,
            dma, dma, dma, dma, dma, dma, pltpu.SemaphoreType.REGULAR((5,)),
        ],
        compiler_params=pltpu.CompilerParams(collective_id=0, has_side_effects=True, vmem_limit_bytes=60 << 20),
        cost_estimate=pl.CostEstimate(flops=4 * ROWS * D * K, bytes_accessed=ROWS * D * 2, transcendentals=0),
        name="reduce_project_gram",
    )(activations, start_basis)


def factor_kernel(gram_ref, img_ref, basis_ref, r_ref):
    g = [jnp.concatenate([gram_ref[i][:, :K], gram_ref[i][:, K:]], axis=0) for i in range(8)]
    w = [img_ref[8 * i:8 * i + 8, :] for i in range(8)]
    sub = lax.broadcasted_iota(jnp.int32, (8, 128), 0)
    lane = lax.broadcasted_iota(jnp.int32, (8, K), 1)
    row = lax.broadcasted_iota(jnp.int32, (8, K), 0)
    for n in range(8):
        col = [[jnp.broadcast_to(g[i][:, 8 * n + k:8 * n + k + 1], (8, 128)) for i in range(n, 8)] for k in range(8)]
        at = {(h, k): jnp.broadcast_to(col[k][0][h:h + 1, :], (8, 128)) for k in range(8) for h in range(k + 1)}
        scale = jnp.zeros((8, 128), F32)
        for k in range(8):
            inv = 1.0 / at[k, k]
            scale = jnp.where(sub == k, at[k, k], scale)
            m = [c * inv for c in col[k]]
            m[0] = jnp.where(sub > k, m[0], 0.0)
            for k2 in range(k + 1, 8):
                f = at[k, k2] * inv
                for k1 in range(k + 1, k2 + 1):
                    at[k1, k2] = at[k1, k2] - at[k, k1] * f
                for i in range(8 - n):
                    col[k2][i] = col[k2][i] - m[i] * at[k, k2]
            gp = jnp.broadcast_to(g[n][k:k + 1, :], (8, K))
            wp = jnp.broadcast_to(w[n][k:k + 1, :], (8, ROWS))
            for i in range(n, 8):
                g[i] = g[i] - m[i - n][:, :K] * gp
                w[i] = w[i] - jnp.concatenate([m[i - n], m[i - n]], axis=1) * wp
        root = lax.rsqrt(scale)
        r_ref[8 * n:8 * n + 8, :] = jnp.where(lane >= row + 8 * n, g[n] * root[:, :K], 0.0)
        basis_ref[8 * n:8 * n + 8, :] = w[n] * jnp.concatenate([root, root], axis=1)


def factor(gram, image):
    return pl.pallas_call(
        factor_kernel,
        out_shape=(jax.ShapeDtypeStruct((K, ROWS), F32), jax.ShapeDtypeStruct((K, K), F32)),
        name="cholesky_solve",
    )(gram, image)


def on_device(activations, start_basis):
    image, gram = comm(activations, start_basis.T)
    basis, rfactor = factor(gram, image)
    return (basis.T, rfactor)


def solution(mesh):
    in_specs = (P(("rows", "grp"), None), P(("rows", "grp"), None))
    out_specs = (P(("rows", "grp"), None), P())
    return jax.shard_map(
        on_device, mesh=mesh, in_specs=in_specs, out_specs=out_specs, check_vma=False
    )
```

```python
import functools
import math

import jax
import jax.numpy as jnp
from jax import lax
from jax.experimental import pallas as pl
from jax.experimental.pallas import tpu as pltpu
from jax.sharding import PartitionSpec as P

MESH = pl.DeviceIdType.MESH
F32 = jnp.float32
BF16 = jnp.bfloat16
ROWS, D, K = 256, 8192, 64
TOTAL = 131072
OWNERS = ((3, 13, 8, 9, 5, 7, 11, 10), (14, 6, 8, 9, 4, 12, 11, 10))
CHUNK = 512


def comm_kernel(a_hbm, s_hbm, img_ref, gram_ref, a_v, s_v, other, land_c, r1, out_1, land_1, r2, land_2, r3, land_z, pall,
                g_own, land_g, g_z, g_all,
                load_sem, c_send, c_recv, s1_send, s1_recv, s2_send, s2_recv, z_send, z_recv,
                zg_send, zg_recv, xy_send, xy_recv, f_send, f_recv,
                g1_send, g1_recv, g2_send, g2_recv, g3_send, g3_recv, know):
    r = lax.axis_index("rows")
    g = lax.axis_index("grp")
    x, z = r // 16, r % 16
    y, c = g // 2, g % 2

    def dev(xx, yy, zz, cc):
        return (xx * 16 + zz, yy * 2 + cc)

    partner = dev(x, y, z, 1 - c)

    def plane(k):
        return (x + k // 8) % 4, (y + (k // 2) % 4) % 4, (c + k % 2) % 2

    def remote(src, dst, ss, rs, target):
        return pltpu.make_async_remote_copy(src_ref=src, dst_ref=dst, send_sem=ss, recv_sem=rs, device_id=target,
                                            device_id_type=MESH)

    def arrived(ref, sem):
        pltpu.make_async_copy(ref, ref, sem).wait()

    me_a = (x, y)
    me_b = (y, x)
    steps = (2, 1, 3, 0)

    def chunk(half, q, t):
        return (c if half == 0 else 1 - c) * 8 + q * 4 + (me_a[q] + steps[t]) % 4

    def load(half, q, t):
        ch = chunk(half, q, t)
        src = a_hbm.at[:, pl.ds(pl.multiple_of(ch * CHUNK, CHUNK), CHUNK)]
        return pltpu.make_async_copy(src, a_v.at[ch], load_sem.at[t])

    bar = pltpu.get_barrier_semaphore()
    x_peers = [dev((x + k) % 4, y, z, c) for k in (1, 2, 3)]
    y_peers = [dev(x, (y + k) % 4, z, c) for k in (1, 2, 3)]

    def z_peers(k):
        return [dev(x, y, (z + k) % 16, c), dev(x, y, (z + 16 - k) % 16, c)]

    def greet(sem, targets):
        for target in targets:
            pl.semaphore_signal(sem, inc=1, device_id=target, device_id_type=MESH)

    greet(bar, [partner] + x_peers + y_peers + z_peers(1))

    load_s = pltpu.make_async_copy(s_hbm, s_v, load_sem.at[4])
    load_s.start()
    for t in range(4):
        for half in (1, 0):
            for q in range(2):
                load(half, q, t).start()

    load_s.wait()
    st = s_v[...]

    def partial(half, q, t, dst):
        part = jnp.dot(st, a_v[chunk(half, q, t)], preferred_element_type=F32)
        for s in range(4):
            for b in range(4):
                dst[q * 4 + s, (me_a[q] + steps[t]) % 4, b] = part[16 * s:16 * s + 16, 128 * b:128 * b + 128]

    def first_peer(q, k):
        return dev((x + k) % 4, y, z, c) if q == 0 else dev(x, (y + k) % 4, z, c)

    def second_peer(q, k):
        return first_peer(1 - q, k)

    def c_copy(q, t):
        a = (me_a[q] + steps[t]) % 4
        four = pl.ds(q * 4, 4)
        return remote(other.at[four, a], land_c.at[four, a], c_send, c_recv.at[t], partner)

    def first_axis(t):
        k = steps[t]
        arrived(land_c.at[pl.ds(0, 2)], c_recv.at[t])
        for q in range(2):
            a = (me_a[q] + k) % 4
            for s in range(4):
                i = q * 4 + s
                part = r1[i, a] + land_c[i, a]
                if k == 0:
                    r1[i, a] = part
                else:
                    out_1[i, a] = part.astype(BF16)
                    remote(out_1.at[i, a], land_1.at[i, k - 1], s1_send, s1_recv.at[s], first_peer(q, k)).start()

    for t in range(4):
        arrived(a_v.at[pl.ds(0, 4)], load_sem.at[t])
        for q in range(2):
            partial(1, q, t, other)
        for q in range(2):
            partial(0, q, t, r1)
        if t == 0:
            pl.semaphore_wait(bar, 9)
        for q in range(2):
            c_copy(q, t).start()
        if t == 0:
            greet(know.at[0], y_peers)
            greet(know.at[1], z_peers(1))
        if t >= 1:
            first_axis(t - 1)
        if t == 3:
            pl.semaphore_wait(know.at[0], 3)
            greet(know.at[2], [partner])
            pl.semaphore_wait(know.at[1], 2)
            greet(know.at[3], z_peers(2))
    first_axis(3)
    pl.semaphore_wait(know.at[3], 2)
    greet(know.at[4], z_peers(4))

    for s in range(4):
        arrived(land_1.at[pl.ds(0, 2)], s1_recv.at[s])
        for q in range(2):
            i = q * 4 + s
            r2[i] = (r1[i, me_a[q]] + land_1[i, 0].astype(F32)) + (land_1[i, 1].astype(F32) + land_1[i, 2].astype(F32))
            for k in (1, 2, 3):
                remote(r2.at[i, (me_b[q] + k) % 4], land_2.at[i, k - 1], s2_send, s2_recv.at[s], second_peer(q, k)).start()

    owners = [jnp.where(c == 0, OWNERS[0][i], OWNERS[1][i]) for i in range(8)]

    def z_copy(i, slot):
        zo = owners[i]
        return remote(r3.at[i], land_z.at[slot], z_send, z_recv, dev(x, y, zo, c))

    for s in range(4):
        arrived(land_2.at[pl.ds(0, 2)], s2_recv.at[s])
        for q in range(2):
            i = q * 4 + s
            r3[i] = (r2[i, me_b[q]] + land_2[i, 0]) + (land_2[i, 1] + land_2[i, 2])
            if i == 0:
                pl.semaphore_wait(know.at[4], 2)
            zo = owners[i]

            @pl.when(zo != z)
            def _(i=i, zo=zo):
                z_copy(i, (zo - z + 16) % 16).start()

    my_i = sum(jnp.where(owners[i] == z, i, 0) for i in range(8))
    my_s, my_q = my_i % 4, my_i // 4
    owner = sum(jnp.where(owners[i] == z, 1, 0) for i in range(8)) == 1

    def place(q):
        return (c * 2 + q) * 16 + jnp.where(q == 0, x * 4 + y, y * 4 + x)

    def zg_copy(k):
        here = pall.at[place(my_q), my_s]
        return remote(here, here, zg_send, zg_recv.at[my_i], dev(x, y, (z + k) % 16, c))

    @pl.when(owner)
    def _():
        total = r3[my_i]
        arrived(land_z.at[pl.ds(1, 15)], z_recv)
        for k in range(1, 16):
            total = total + land_z[k]
        pall[place(my_q), my_s] = (total * (1.0 / math.sqrt(TOTAL))).astype(BF16)

        for k in (8, 7, 9, 6, 10, 5, 11, 4, 12, 3, 13, 2, 14, 1, 15):
            zg_copy(k).start()

    def far(k):
        return min(k // 4, 4 - k // 4) + min(k % 4, 4 - k % 4)

    def xy_copy(k, q, s):
        here = pall.at[place(q), s]
        return remote(here, here, xy_send, xy_recv.at[far(k) - 1], dev((x + k // 4) % 4, (y + k % 4) % 4, z, c))

    for i in (6, 7, 3, 2, 1, 5, 4, 0):
        q, s = i // 4, i % 4

        @pl.when(z != owners[i])
        def _(s=s, q=q):
            arrived(pall.at[place(q), s], zg_recv.at[q * 4 + s])

        for k in range(1, 16):
            xy_copy(k, q, s).start()

    def forward(k, q):
        xx, yy = (x - k // 4 + 4) % 4, (y - k % 4 + 4) % 4
        p = (c * 2 + q) * 16 + (xx * 4 + yy if q == 0 else yy * 4 + xx)
        return remote(pall.at[p], pall.at[p], f_send, f_recv, partner)

    for q in range(2):
        forward(0, q).start()

    for hops in range(1, 5):
        ring = [k for k in range(1, 16) if far(k) == hops]
        arrived(pall.at[pl.ds(0, 2 * len(ring))], xy_recv.at[hops - 1])
        for k in ring:
            for q in range(2):
                forward(k, q).start()

    def image_part(half, acc):
        for j in range(8):
            ch = half * 8 + j
            pt = jnp.concatenate([pall[ch * 4 + b].reshape(64, 128) for b in range(4)], axis=1)
            acc = acc + lax.dot_general(pt, a_v[ch], (((1,), (1,)), ((), ())), preferred_element_type=F32)
        return acc

    acc = image_part(c, jnp.zeros((K, ROWS), F32))
    theirs = pall.at[pl.ds((1 - c) * 32, 32)]
    arrived(theirs, f_recv)
    acc = image_part(1 - c, acc)
    img = acc * (1.0 / math.sqrt(D))
    img_ref[...] = img
    gram = lax.dot_general(img, img, (((1,), (1,)), ((), ())), precision=lax.Precision.HIGHEST, preferred_element_type=F32)
    gram = gram * (1.0 / TOTAL)

    for m in range(8):
        g_own[m] = jnp.concatenate([gram[8 * m:8 * m + 4, :], gram[8 * m + 4:8 * m + 8, :]], axis=1)
    me = y * 2 + c
    seat = x * 8 + me

    def g1_copy(k):
        xx, yy, cc = plane(k)
        return remote(g_own.at[yy * 2 + cc], land_g.at[seat], g1_send, g1_recv, dev(xx, yy, z, cc))

    pl.semaphore_wait(know.at[2], 1)
    for k in range(1, 32):
        g1_copy(k).start()

    arrived(other, c_send)
    arrived(out_1.at[pl.ds(0, 6)], s1_send)
    arrived(r2.at[pl.ds(0, 6)], s2_send)

    @pl.when(owner)
    def _():
        arrived(r3.at[pl.ds(0, 7)], z_send)
        arrived(land_z.at[pl.ds(0, 15), pl.ds(0, 8)], zg_send)

    @pl.when(jnp.logical_not(owner))
    def _():
        arrived(r3, z_send)

    arrived(pall.at[pl.ds(0, 30)], xy_send)
    arrived(theirs, f_send)

    land_g[seat] = g_own[me]
    most = land_g.at[pl.ds(0, 31)]
    arrived(most, g1_recv)
    g_z[z] = jnp.sum(land_g[...], axis=0)

    def g2_copy(k):
        return remote(g_z.at[z], g_z.at[z], g2_send, g2_recv, dev(x, y, (z + k) % 16, c))

    for k in (8, 7, 9, 6, 10, 5, 11, 4, 12, 3, 13, 2, 14, 1, 15):
        g2_copy(k).start()
    arrived(most, g1_send)
    line = g_z.at[pl.ds(0, 15)]
    arrived(line, g2_recv)
    g_all[me] = jnp.sum(g_z[...], axis=0)

    def g3_copy(k):
        xx, yy, cc = plane(k)
        return remote(g_all.at[me], g_all.at[me], g3_send, g3_recv, dev(xx, yy, z, cc))

    for k in range(1, 8):
        g3_copy(k).start()
    arrived(line, g2_send)
    others = g_all.at[pl.ds(0, 7)]
    arrived(others, g3_recv)
    gram_ref[...] = g_all[...]
    arrived(others, g3_send)


def comm(activations, start_basis):
    dma = pltpu.SemaphoreType.DMA
    return pl.pallas_call(
        comm_kernel,
        out_shape=(jax.ShapeDtypeStruct((K, ROWS), F32), jax.ShapeDtypeStruct((8, 4, 128), F32)),
        in_specs=[pl.BlockSpec(memory_space=pl.ANY)] * 2,
        out_specs=(pl.BlockSpec(memory_space=pltpu.VMEM),) * 2,
        scratch_shapes=[
            pltpu.VMEM((16, ROWS, CHUNK), BF16),
            pltpu.VMEM((K, ROWS), BF16),
            pltpu.VMEM((8, 4, 4, 16, 128), F32),
            pltpu.VMEM((8, 4, 4, 16, 128), F32),
            pltpu.VMEM((8, 4, 4, 16, 128), F32),
            pltpu.VMEM((8, 4, 4, 16, 128), BF16),
            pltpu.VMEM((8, 3, 4, 16, 128), BF16),
            pltpu.VMEM((8, 4, 16, 128), F32),
            pltpu.VMEM((8, 3, 16, 128), F32),
            pltpu.VMEM((8, 16, 128), F32),
            pltpu.VMEM((16, 16, 128), F32),
            pltpu.VMEM((64, 4, 16, 128), BF16),
            pltpu.VMEM((8, 4, 128), F32),
            pltpu.VMEM((32, 4, 128), F32),
            pltpu.VMEM((16, 4, 128), F32),
            pltpu.VMEM((8, 4, 128), F32),
            dma((5,)), dma, dma((4,)), dma, dma((4,)), dma, dma((4,)), dma, dma,
            dma, dma((8,)), dma, dma((4,)), dma, dma,
            dma, dma, dma, dma, dma, dma, pltpu.SemaphoreType.REGULAR((5,)),
        ],
        compiler_params=pltpu.CompilerParams(collective_id=0, has_side_effects=True, vmem_limit_bytes=60 << 20),
        cost_estimate=pl.CostEstimate(flops=4 * ROWS * D * K, bytes_accessed=ROWS * D * 2, transcendentals=0),
        name="reduce_project_gram",
    )(activations, start_basis)


def factor_kernel(gram_ref, img_ref, basis_ref, r_ref):
    g = [jnp.concatenate([gram_ref[i][:, :K], gram_ref[i][:, K:]], axis=0) for i in range(8)]
    w = [img_ref[8 * i:8 * i + 8, :] for i in range(8)]
    sub = lax.broadcasted_iota(jnp.int32, (8, 128), 0)
    lane = lax.broadcasted_iota(jnp.int32, (8, K), 1)
    row = lax.broadcasted_iota(jnp.int32, (8, K), 0)
    for n in range(8):
        col = [[jnp.broadcast_to(g[i][:, 8 * n + k:8 * n + k + 1], (8, 128)) for i in range(n, 8)] for k in range(8)]
        at = {(h, k): jnp.broadcast_to(col[k][0][h:h + 1, :], (8, 128)) for k in range(8) for h in range(k + 1)}
        scale = jnp.zeros((8, 128), F32)
        for k in range(8):
            inv = 1.0 / at[k, k]
            scale = jnp.where(sub == k, at[k, k], scale)
            m = [c * inv for c in col[k]]
            m[0] = jnp.where(sub > k, m[0], 0.0)
            for k2 in range(k + 1, 8):
                f = at[k, k2] * inv
                for k1 in range(k + 1, k2 + 1):
                    at[k1, k2] = at[k1, k2] - at[k, k1] * f
                for i in range(8 - n):
                    col[k2][i] = col[k2][i] - m[i] * at[k, k2]
            gp = jnp.broadcast_to(g[n][k:k + 1, :], (8, K))
            wp = jnp.broadcast_to(w[n][k:k + 1, :], (8, ROWS))
            for i in range(n, 8):
                g[i] = g[i] - m[i - n][:, :K] * gp
                w[i] = w[i] - jnp.concatenate([m[i - n], m[i - n]], axis=1) * wp
        root = lax.rsqrt(scale)
        r_ref[8 * n:8 * n + 8, :] = jnp.where(lane >= row + 8 * n, g[n] * root[:, :K], 0.0)
        basis_ref[8 * n:8 * n + 8, :] = w[n] * jnp.concatenate([root, root], axis=1)


def factor(gram, image):
    return pl.pallas_call(
        factor_kernel,
        out_shape=(jax.ShapeDtypeStruct((K, ROWS), F32), jax.ShapeDtypeStruct((K, K), F32)),
        name="cholesky_solve",
    )(gram, image)


def on_device(activations, start_basis):
    image, gram = comm(activations, start_basis.T)
    basis, rfactor = factor(gram, image)
    return (basis.T, rfactor)


def solution(mesh):
    in_specs = (P(("rows", "grp"), None), P(("rows", "grp"), None))
    out_specs = (P(("rows", "grp"), None), P())
    return jax.shard_map(
        on_device, mesh=mesh, in_specs=in_specs, out_specs=out_specs, check_vma=False
    )
```
